256 devices in a mesh: gx: 32 (over z, y), gy: 8 (over x, core).
Axes of the slice: x: 4, y: 4, z: 8, core: 2. Of those that a mesh axis runs over, the one named last changes fastest.
Arguments:
- load_vector: float32 [64, 16, 192, 128], P('gx', 'gy'), may hold values from -6 to 6
- blocks: bfloat16 [4, 64, 16, 192, 192], P(None, 'gx', 'gy'), may hold values from -11 to 13
Outputs:
- solution: float32 [64, 16, 192, 128], P('gx', 'gy')
The draws below stay inside these ranges and needn't reach their ends.
All inputs are finite; a program needn't handle non-finite values.
Results may differ from the reference program's by a relative error of at most 0.0038.
Values may be sent and summed in bfloat16 or wider, within the bound.
A program may use at most 64 MiB of HBM per device.

```python
import jax
import jax.numpy as jnp
from jax import lax

B = 192
R = 128
CX = 2
CY = 2
OV = 1
SWEEPS = 2
ITERS = 2
NX = 64
NY = 16
N_GX = 32
N_GY = 8


def draw_load_vector(key, part):
    key = jax.random.fold_in(key, 11)
    noise_key, length_key, width_key = jax.random.split(key, 3)
    full_shape = (NX, NY, B, R)
    noise = jnp.clip(jax.random.normal(noise_key, full_shape, jnp.float32), -6.0, 6.0)
    length_rate = jax.random.uniform(length_key, (1, 1, 1, R), jnp.float32, -3.0, 3.0)
    width_rate = jax.random.uniform(width_key, (1, 1, 1, R), jnp.float32, -2.0, 2.0)
    length_place = lax.broadcasted_iota(jnp.int32, (NX, 1, 1, 1), 0).astype(jnp.float32) / (NX - 1.0) - 0.5
    width_place = lax.broadcasted_iota(jnp.int32, (1, NY, 1, 1), 1).astype(jnp.float32) / (NY - 1.0) - 0.5
    exponent = length_rate * length_place + width_rate * width_place - 0.5 * (jnp.abs(length_rate) + jnp.abs(width_rate))
    return noise * jnp.exp(exponent)


def draw_blocks(key, part):
    key = jax.random.fold_in(key, 5)
    noise_key, scale_key, spread_key = jax.random.split(key, 3)
    full_shape = (4, NX, NY, B, B)
    noise = jnp.clip(jax.random.normal(noise_key, full_shape, jnp.float32), -4.0, 4.0)
    rise = 2.0
    width_place = lax.broadcasted_iota(jnp.int32, (1, NY, 1, 1), 1).astype(jnp.float32) / (NY - 1.0)
    scale_draw = jax.random.uniform(scale_key, (NX, NY, 1, 1), jnp.float32, 0.0, 1.0)
    node_scale = 6.0 * jnp.exp(jnp.log(2.0) * (0.8 * width_place + 0.2 * scale_draw))
    coupling_scale = jnp.exp(jax.random.uniform(spread_key, (2, NX, NY, 1, 1), jnp.float32, jnp.log(0.5), jnp.log(1.5)))
    width_factor = 1.2 - 0.4 * width_place
    position = lax.broadcasted_iota(jnp.int32, (NX, 1, 1, 1), 0).astype(jnp.float32)
    ramp = 1.0 + rise * position / (NX - 1.0)
    row_index = lax.broadcasted_iota(jnp.int32, (B, B), 0)
    column_index = lax.broadcasted_iota(jnp.int32, (B, B), 1)
    identity = (row_index == column_index).astype(jnp.float32)
    diagonal_block = node_scale * identity + 0.015 * node_scale * noise[0]
    couplings = 0.36 / jnp.sqrt(B * 1.0) * coupling_scale * ramp * width_factor * noise[1:3]
    smoother = (identity + 0.02 * noise[3]) / node_scale
    return jnp.concatenate([diagonal_block[None], couplings, smoother[None]], axis=0).astype(jnp.bfloat16)


def setup_inputs(seed: int = 0) -> dict:
    seeds = jax.random.split(jax.random.key(seed), 3)
    return {
        "load_vector": draw_load_vector(jax.random.fold_in(seeds[2], 71), 0),
        "blocks": draw_blocks(jax.random.fold_in(seeds[2], 71), 0),
    }


def local_product(matrices, operand):
    return jnp.einsum('xyij,xyjr->xyir', matrices.astype(jnp.float32), operand.astype(jnp.float32))

def local_transposed(matrices, operand):
    return jnp.einsum('xyji,xyjr->xyir', matrices.astype(jnp.float32), operand.astype(jnp.float32))

def couple_box(blocks, operand):
    total = local_product(blocks[0], operand)
    total = total + local_product(blocks[1], jnp.pad(operand[1:], ((0, 1), (0, 0), (0, 0), (0, 0))))
    total = total + jnp.pad(local_transposed(blocks[1], operand)[:-1], ((1, 0), (0, 0), (0, 0), (0, 0)))
    total = total + local_product(blocks[2], jnp.pad(operand[:, 1:], ((0, 0), (0, 1), (0, 0), (0, 0))))
    total = total + jnp.pad(local_transposed(blocks[2], operand)[:, :-1], ((0, 0), (1, 0), (0, 0), (0, 0)))
    return total

def smooth_box(blocks, values):
    smoothed = local_product(blocks[3], values.astype(jnp.bfloat16))
    for sweep_index in range(SWEEPS - 1):
        defect = values - couple_box(blocks, smoothed.astype(jnp.bfloat16))
        smoothed = smoothed + local_product(blocks[3], defect.astype(jnp.bfloat16))
    return smoothed

def precondition(padded_blocks, vector):
    padded_vector = jnp.pad(vector, ((OV, OV), (OV, OV), (0, 0), (0, 0)))

    def one_domain(device_index):
        start_first = (device_index // N_GY * CX).astype(jnp.int32)
        start_second = (device_index % N_GY * CY).astype(jnp.int32)
        anchor = jnp.zeros((), jnp.int32)
        local_blocks = lax.dynamic_slice(padded_blocks, (anchor, start_first, start_second, anchor, anchor), (4, CX + 2 * OV, CY + 2 * OV, B, B))
        local_vector = lax.dynamic_slice(padded_vector, (start_first, start_second, anchor, anchor), (CX + 2 * OV, CY + 2 * OV, B, R))
        smoothed = smooth_box(local_blocks, local_vector)
        return smoothed[OV:OV + CX, OV:OV + CY]
    pieces = lax.map(one_domain, jnp.arange(N_GX * N_GY, dtype=jnp.int32))
    pieces = pieces.reshape(N_GX, N_GY, CX, CY, B, R)
    return pieces.transpose(0, 2, 1, 3, 4, 5).reshape(NX, NY, B, R)

def rotate_solve(columns, initial_norm):
    column_count = len(columns)
    targets = [initial_norm] + [jnp.zeros_like(initial_norm) for position in range(column_count)]
    cosines = []
    sine_list = []
    triangle = []
    for column_index in range(column_count):
        entries = list(columns[column_index])
        for earlier in range(column_index):
            upper_entry = cosines[earlier] * entries[earlier] + sine_list[earlier] * entries[earlier + 1]
            lower_entry = cosines[earlier] * entries[earlier + 1] - sine_list[earlier] * entries[earlier]
            entries[earlier] = upper_entry
            entries[earlier + 1] = lower_entry
        radius = jnp.sqrt(entries[column_index] * entries[column_index] + entries[column_index + 1] * entries[column_index + 1])
        cosine = entries[column_index] / radius
        sine = entries[column_index + 1] / radius
        entries[column_index] = radius
        cosines.append(cosine)
        sine_list.append(sine)
        lower_target = -sine * targets[column_index]
        targets[column_index] = cosine * targets[column_index]
        targets[column_index + 1] = lower_target
        triangle.append(entries[:column_index + 1])
    weights = [None] * column_count
    for column_index in reversed(range(column_count)):
        running = targets[column_index]
        for later in range(column_index + 1, column_count):
            running = running - triangle[later][column_index] * weights[later]
        weights[column_index] = running / triangle[column_index][column_index]
    return weights

def reference(load_vector, blocks):
    padded_blocks = jnp.pad(blocks, ((0, 0), (OV, OV), (OV, OV), (0, 0), (0, 0)))
    initial_norm = jnp.sqrt(lax.optimization_barrier(jnp.sum(load_vector * load_vector, axis=(0, 1, 2))))
    krylov_basis = [load_vector / initial_norm]
    corrections = []
    columns = []
    for iteration in range(ITERS):
        correction = precondition(padded_blocks, krylov_basis[iteration])
        corrections.append(correction)
        product_vector = couple_box(blocks, correction.astype(jnp.bfloat16))
        heights = [lax.optimization_barrier(jnp.sum(vector * product_vector, axis=(0, 1, 2))) for vector in krylov_basis]
        for position in range(len(heights)):
            product_vector = product_vector - heights[position] * krylov_basis[position]
        subdiagonal = jnp.sqrt(lax.optimization_barrier(jnp.sum(product_vector * product_vector, axis=(0, 1, 2))))
        columns.append(heights + [subdiagonal])
        if iteration + 1 < ITERS:
            krylov_basis.append(product_vector / subdiagonal)
    weights = rotate_solve(columns, initial_norm)
    solution = weights[0] * corrections[0]
    for position in range(1, ITERS):
        solution = solution + weights[position] * corrections[position]
    return solution
```

```python
import functools

import jax
import jax.numpy as jnp
from jax import lax
from jax.experimental import pallas as pl
from jax.experimental.pallas import tpu as pltpu
from jax.sharding import PartitionSpec as P

MESH = pl.DeviceIdType.MESH
F32 = jnp.float32
BF16 = jnp.bfloat16
NODES = [(0, 0), (0, 1), (1, 0), (1, 1)]
XL, XH, YL, YH = range(4)
SUMS = 3
TERMS = 4


def dot(a, b):
    return jnp.dot(a, b, preferred_element_type=F32)


def split(u):
    high = u.astype(BF16)
    return high, (u - high.astype(F32)).astype(BF16)


def dot2(a, u):
    high, low = split(u)
    return dot(a, high) + dot(a, low)


def over_rows(a):
    return jnp.sum(a, axis=0, keepdims=True)


def kernel(
    ngx, ngy, fast,
    load_ref, blocks_ref, out_ref,
    v, m, t1, t2, sent, products, halo, first, total, c1, c2, w, q,
    mine, landed,
    load_sem, halo_send, halo_recv, sum_send, sum_recv,
):
    gx, gy = lax.axis_index("gx"), lax.axis_index("gy")
    up_x, down_x = lax.rem(gx + 1, ngx), lax.rem(gx + ngx - 1, ngx)
    up_y, down_y = lax.rem(gy + 1, ngy), lax.rem(gy + ngy - 1, ngy)
    sides = {XL: (up_x, gy), XH: (down_x, gy), YL: (gx, up_y), YH: (gx, down_y)}

    slow = ngx // fast
    chips = ngy // 2
    along, across = gx // fast, gx % fast
    chip, core = gy // 2, gy % 2
    groups = [
        [
            (lax.rem(along + d, slow) * fast + across, chip * 2 + lax.rem(core + e, 2))
            for d in range(slow)
            for e in range(2)
            if d or e
        ],
        [
            (along * fast + lax.rem(across + d, fast), lax.rem(chip + e, chips) * 2 + core)
            for d in range(fast)
            for e in range(chips)
            if d or e
        ],
    ]

    loads = [
        pltpu.make_async_copy(load_ref, v, load_sem.at[0]),
        pltpu.make_async_copy(blocks_ref.at[3], m.at[3], load_sem.at[1]),
        pltpu.make_async_copy(blocks_ref.at[1], m.at[1], load_sem.at[2]),
        pltpu.make_async_copy(blocks_ref.at[2], m.at[2], load_sem.at[3]),
        pltpu.make_async_copy(blocks_ref.at[0], m.at[0], load_sem.at[4]),
    ]
    for copy in loads:
        copy.start()

    barrier = pltpu.get_barrier_semaphore()
    partners = [*sides.values(), *groups[0], *groups[1]]
    for partner in partners:
        pl.semaphore_signal(barrier, inc=1, device_id=partner, device_id_type=MESH)

    started = []

    def send(source, step, side, place):
        slot = side * 2 + place
        copy = pltpu.make_async_remote_copy(
            src_ref=source,
            dst_ref=halo.at[step, side, place],
            send_sem=halo_send.at[step, slot],
            recv_sem=halo_recv.at[step, slot],
            device_id=sides[side],
            device_id_type=MESH,
        )
        copy.start()
        started.append(copy)
        arriving[step, side, place] = copy

    arriving = {}
    spreading = {}

    def exchange(step, field):
        for i, j in NODES:
            sent[step, i, j] = field[i, j].astype(BF16)
            if i == 0:
                send(sent.at[step, i, j], step, XH, j)
        for j in range(2):
            products[step, 0, j] = dot2(t1[1, j], field[1, j]).astype(BF16)
            send(products.at[step, 0, j], step, XL, j)
        for i in range(2):
            send(sent.at[step, i, 0], step, YH, i)
        for i in range(2):
            products[step, 1, i] = dot2(t2[i, 1], field[i, 1]).astype(BF16)
            send(products.at[step, 1, i], step, YL, i)

    def inner(step, field):
        for i, j in NODES:
            value = dot2(m[0, i, j], field[i, j])
            value += dot(m[1, 0, j], sent[step, 1, j]) if i == 0 else dot(t1[0, j], sent[step, 0, j])
            value += dot(m[2, i, 0], sent[step, i, 1]) if j == 0 else dot(t2[i, 0], sent[step, i, 0])
            total[i, j] = value

    def outer(step, i, j):
        value = total[i, j]
        if j == 0:
            arriving[step, YL, i].wait_recv()
            value += halo[step, YL, i].astype(F32)
        else:
            arriving[step, YH, i].wait_recv()
            value += dot(m[2, i, 1], halo[step, YH, i])
        if i == 0:
            arriving[step, XL, j].wait_recv()
            value += halo[step, XL, j].astype(F32)
        else:
            arriving[step, XH, j].wait_recv()
            value += dot(m[1, 1, j], halo[step, XH, j])
        return value

    def spread(number, phase, rows):
        for term, row in enumerate(rows):
            mine[number, phase, pl.ds(term, 1)] = row
        copies = []
        for slot, partner in enumerate(groups[phase]):
            copy = pltpu.make_async_remote_copy(
                src_ref=mine.at[number, phase],
                dst_ref=landed.at[number, phase, slot],
                send_sem=sum_send.at[number, phase, slot],
                recv_sem=sum_recv.at[number, phase, slot],
                device_id=partner,
                device_id_type=MESH,
            )
            copy.start()
            copies.append(copy)
        started.extend(copies)
        spreading[number, phase] = copies

    def gather(number, phase, count):
        value = mine[number, phase]
        for slot, copy in enumerate(spreading[number, phase]):
            copy.wait_recv()
            value += landed[number, phase, slot]
        return [value[term : term + 1] for term in range(count)]

    def inner_products(*pairs):
        rows = []
        for a, b in pairs:
            row = None
            for i, j in NODES:
                part = over_rows(a[i, j] * b[i, j])
                row = part if row is None else row + part
            rows.append(row)
        return rows

    for number in range(SUMS):
        for phase in range(2):
            mine[number, phase] = jnp.zeros_like(mine[number, phase])

    loads[2].wait()
    loads[3].wait()

    @pl.when(gx == ngx - 1)
    def _():
        for j in range(2):
            m[1, 1, j] = jnp.zeros_like(m[1, 1, j])

    @pl.when(gy == ngy - 1)
    def _():
        for i in range(2):
            m[2, i, 1] = jnp.zeros_like(m[2, i, 1])

    for i, j in NODES:
        t1[i, j] = m[1, i, j].T
        t2[i, j] = m[2, i, j].T

    loads[0].wait()
    loads[1].wait()
    for i, j in NODES:
        first[i, j] = dot2(m[3, i, j], v[i, j])
    pl.semaphore_wait(barrier, len(partners))
    exchange(0, first)
    spread(0, 0, inner_products((v, v)))
    loads[4].wait()
    inner(0, first)
    for i, j in NODES:
        c1[i, j] = first[i, j] + dot2(m[3, i, j], v[i, j] - outer(0, i, j))
    exchange(1, c1)
    spread(0, 1, gather(0, 0, 1))
    inner(1, c1)
    (square,) = gather(0, 1, 1)
    norm = jnp.sqrt(square)
    for i, j in NODES:
        w[i, j] = outer(1, i, j) / norm
        first[i, j] = dot2(m[3, i, j], w[i, j])
    exchange(2, first)
    for i, j in NODES:
        v[i, j] = v[i, j] / norm
    spread(1, 0, inner_products((w, w), (w, v)))
    inner(2, first)
    for i, j in NODES:
        c2[i, j] = first[i, j] + dot2(m[3, i, j], w[i, j] - outer(2, i, j))
    exchange(3, c2)
    spread(1, 1, gather(1, 0, 2))
    inner(3, c2)
    ww, wb = gather(1, 1, 2)
    size = jnp.sqrt(ww)
    scale = 1.0 / size
    for i, j in NODES:
        q[i, j] = outer(3, i, j) * scale
    spread(2, 0, inner_products((w, q), (q, q), (v, q)))
    spread(2, 1, gather(2, 0, 3))
    wq, qq, bq = gather(2, 1, 3)
    wq = wq * scale
    wb = wb * scale
    second = (bq - wq * wb) / (qq - wq * wq)
    weight_1 = (wb - wq * second) * scale
    weight_2 = second * scale * norm
    for i, j in NODES:
        out_ref[i, j] = weight_1 * c1[i, j] + weight_2 * c2[i, j]
    for copy in started:
        copy.wait_send()


def solution(mesh):
    ngx, ngy = mesh.shape["gx"], mesh.shape["gy"]
    fast = 4

    def local(load_vector, blocks):
        cx, cy, size, cases = load_vector.shape
        field = (cx, cy, size, cases)
        matrices = (cx, cy, size, size)
        sem = pltpu.SemaphoreType.DMA
        return pl.pallas_call(
            functools.partial(kernel, ngx, ngy, fast),
            out_shape=jax.ShapeDtypeStruct(field, F32),
            in_specs=[pl.BlockSpec(memory_space=pl.ANY)] * 2,
            out_specs=pl.BlockSpec(memory_space=pltpu.VMEM),
            scratch_shapes=[
                pltpu.VMEM(field, F32),
                pltpu.VMEM((4, *matrices), BF16),
                pltpu.VMEM(matrices, BF16),
                pltpu.VMEM(matrices, BF16),
                pltpu.VMEM((4, *field), BF16),
                pltpu.VMEM((4, 2, 2, size, cases), BF16),
                pltpu.VMEM((4, 4, 2, size, cases), BF16),
                pltpu.VMEM(field, F32),
                pltpu.VMEM(field, F32),
                pltpu.VMEM(field, F32),
                pltpu.VMEM(field, F32),
                pltpu.VMEM(field, F32),
                pltpu.VMEM(field, F32),
                pltpu.VMEM((SUMS, 2, TERMS, cases), F32),
                pltpu.VMEM((SUMS, 2, 15, TERMS, cases), F32),
                sem((5,)),
                sem((4, 8)),
                sem((4, 8)),
                sem((SUMS, 2, 15)),
                sem((SUMS, 2, 15)),
            ],
            compiler_params=pltpu.CompilerParams(
                collective_id=0, has_side_effects=True, vmem_limit_bytes=48 * 1024 * 1024
            ),
        )(load_vector, blocks)

    return jax.shard_map(
        local,
        mesh=mesh,
        in_specs=(P("gx", "gy", None, None), P(None, "gx", "gy", None, None)),
        out_specs=P("gx", "gy", None, None),
        check_vma=False,
    )
```

```python
import functools

import jax
import jax.numpy as jnp
from jax import lax
from jax.experimental import pallas as pl
from jax.experimental.pallas import tpu as pltpu
from jax.sharding import PartitionSpec as P

MESH = pl.DeviceIdType.MESH
F32 = jnp.float32
BF16 = jnp.bfloat16
NODES = [(0, 0), (1, 0), (0, 1), (1, 1)]
XL, XH, YL, YH = range(4)
TERMS = (1, 2, 4)


def dot(a, b):
    return jnp.dot(a, b, preferred_element_type=F32)


def split(u):
    high = u.astype(BF16)
    return high, (u - high.astype(F32)).astype(BF16)


def dot2(a, u):
    both = dot(a, jnp.concatenate(split(u), axis=1))
    half = u.shape[1]
    return both[:, :half] + both[:, half:]


def over_rows(a):
    return jnp.sum(a, axis=0, keepdims=True)


def kernel(
    ngx, ngy, fast,
    load_ref, blocks_ref, out_ref,
    v, m, t1, t2, sent, products, halo, first, total, c1, c2, w, q,
    mine_0, mine_1, mine_2, landed_0, landed_1, landed_2,
    load_sem, halo_send, halo_recv, sum_send, sum_recv,
):
    gx, gy = lax.axis_index("gx"), lax.axis_index("gy")
    up_x, down_x = lax.rem(gx + 1, ngx), lax.rem(gx + ngx - 1, ngx)
    up_y, down_y = lax.rem(gy + 1, ngy), lax.rem(gy + ngy - 1, ngy)
    sides = {XL: (up_x, gy), XH: (down_x, gy), YL: (gx, up_y), YH: (gx, down_y)}

    slow = ngx // fast
    chips = ngy // 2
    along, across = gx // fast, gx % fast
    chip, core = gy // 2, gy % 2
    groups = [
        [
            (lax.rem(along + d, slow) * fast + across, chip * 2 + lax.rem(core + e, 2))
            for d in range(slow)
            for e in range(2)
            if d or e
        ],
        [
            (along * fast + lax.rem(across + d, fast), lax.rem(chip + e, chips) * 2 + core)
            for d in range(fast)
            for e in range(chips)
            if d or e
        ],
    ]
    mine = [mine_0, mine_1, mine_2]
    landed = [landed_0, landed_1, landed_2]

    barrier = pltpu.get_barrier_semaphore()
    partners = [*groups[0], *groups[1], *sides.values()]
    for partner in partners:
        pl.semaphore_signal(barrier, inc=1, device_id=partner, device_id_type=MESH)

    loads = [
        pltpu.make_async_copy(load_ref, v, load_sem.at[0]),
        pltpu.make_async_copy(blocks_ref.at[3], m.at[3], load_sem.at[1]),
        pltpu.make_async_copy(blocks_ref.at[1], m.at[1], load_sem.at[2]),
        pltpu.make_async_copy(blocks_ref.at[2], m.at[2], load_sem.at[3]),
        pltpu.make_async_copy(blocks_ref.at[0], m.at[0], load_sem.at[4]),
    ]
    for copy in loads:
        copy.start()

    arriving = {}

    def send(source, step, side, place):
        slot = side * 2 + place
        copy = pltpu.make_async_remote_copy(
            src_ref=source,
            dst_ref=halo.at[step, side, place],
            send_sem=halo_send.at[step, slot],
            recv_sem=halo_recv.at[step, slot],
            device_id=sides[side],
            device_id_type=MESH,
        )
        copy.start()
        arriving[step, side, place] = copy

    def announce(step, i, j):
        if i == 0:
            send(sent.at[step, i, j], step, XH, j)
        if j == 0:
            send(sent.at[step, i, j], step, YH, i)

    def pass_up(step, i, j):
        if i == 1:
            products[step, 0, j] = dot(t1[1, j], sent[step, 1, j]).astype(BF16)
            send(products.at[step, 0, j], step, XL, j)
        if j == 1:
            products[step, 1, i] = dot(t2[i, 1], sent[step, i, 1]).astype(BF16)
            send(products.at[step, 1, i], step, YL, i)

    def exchange(step, field, compute):
        for i, j in NODES:
            value = compute(i, j)
            field[i, j] = value
            sent[step, i, j] = value.astype(BF16)
            announce(step, i, j)
            pass_up(step, i, j)

    def inner(step, field):
        for i, j in NODES:
            value = dot2(m[0, i, j], field[i, j]) if step < 3 else dot(m[0, i, j], sent[step, i, j])
            value += dot(m[1, 0, j], sent[step, 1, j]) if i == 0 else dot(t1[0, j], sent[step, 0, j])
            value += dot(m[2, i, 0], sent[step, i, 1]) if j == 0 else dot(t2[i, 0], sent[step, i, 0])
            total[i, j] = value

    def outer(step, i, j):
        value = total[i, j]
        if j == 0:
            arriving[step, YL, i].wait_recv()
            value += halo[step, YL, i].astype(F32)
        else:
            arriving[step, YH, i].wait_recv()
            value += dot(m[2, i, 1], halo[step, YH, i])
        if i == 0:
            arriving[step, XL, j].wait_recv()
            value += halo[step, XL, j].astype(F32)
        else:
            arriving[step, XH, j].wait_recv()
            value += dot(m[1, 1, j], halo[step, XH, j])
        return value

    def spread(number, phase, rows):
        for term, row in enumerate(rows):
            mine[number][phase, pl.ds(term, 1)] = row
        for slot, partner in enumerate(groups[phase]):
            pltpu.make_async_remote_copy(
                src_ref=mine[number].at[phase],
                dst_ref=landed[number].at[phase, slot],
                send_sem=sum_send.at[number, phase],
                recv_sem=sum_recv.at[number, phase],
                device_id=partner,
                device_id_type=MESH,
            ).start()

    def all_landed(number, phase):
        return pltpu.make_async_remote_copy(
            src_ref=landed[number].at[phase],
            dst_ref=landed[number].at[phase],
            send_sem=sum_send.at[number, phase],
            recv_sem=sum_recv.at[number, phase],
            device_id=groups[phase][0],
            device_id_type=MESH,
        )

    def gather(number, phase, count):
        all_landed(number, phase).wait_recv()
        value = mine[number][phase]
        for slot in range(len(groups[phase])):
            value += landed[number][phase, slot]
        return [value[term : term + 1] for term in range(count)]

    def inner_products(*pairs):
        rows = [None] * len(pairs)
        for i, j in NODES:
            for term, (a, b) in enumerate(pairs):
                part = over_rows(a(i, j) * b(i, j))
                rows[term] = part if rows[term] is None else rows[term] + part
        return rows

    mine_2[...] = jnp.zeros(mine_2.shape, F32)

    loads[0].wait()
    loads[1].wait()
    for i, j in NODES:
        value = dot2(m[3, i, j], v[i, j])
        first[i, j] = value
        sent[0, i, j] = value.astype(BF16)
    pl.semaphore_wait(barrier, len(partners))
    for i, j in NODES:
        announce(0, i, j)
    loads[2].wait()
    loads[3].wait()

    @pl.when(gx == ngx - 1)
    def _():
        for j in range(2):
            m[1, 1, j] = jnp.zeros_like(m[1, 1, j])

    @pl.when(gy == ngy - 1)
    def _():
        for i in range(2):
            m[2, i, 1] = jnp.zeros_like(m[2, i, 1])

    for k in range(2):
        t1[1, k] = m[1, 1, k].T
    for k in range(2):
        t2[k, 1] = m[2, k, 1].T
    for i, j in NODES:
        pass_up(0, i, j)
    spread(0, 0, inner_products((lambda i, j: v[i, j], lambda i, j: v[i, j])))
    for k in range(2):
        t1[0, k] = m[1, 0, k].T
        t2[k, 0] = m[2, k, 0].T
    loads[4].wait()
    inner(0, first)

    exchange(1, c1, lambda i, j: first[i, j] + dot2(m[3, i, j], v[i, j] - outer(0, i, j)))
    inner(1, c1)
    spread(0, 1, gather(0, 0, 1))

    def second_start(i, j):
        w[i, j] = outer(1, i, j)
        return dot2(m[3, i, j], w[i, j])

    exchange(2, first, second_start)
    (square,) = gather(0, 1, 1)
    norm = jnp.sqrt(square)
    inverse = 1.0 / norm
    scaled_w = lambda i, j: w[i, j] * inverse
    scaled_v = lambda i, j: v[i, j] * inverse
    spread(1, 0, inner_products((scaled_w, scaled_w), (scaled_w, scaled_v)))
    inner(2, first)

    exchange(3, c2, lambda i, j: first[i, j] + dot2(m[3, i, j], w[i, j] - outer(2, i, j)))
    inner(3, c2)
    spread(1, 1, gather(1, 0, 2))
    for i, j in NODES:
        q[i, j] = outer(3, i, j)
    ww, wb = gather(1, 1, 2)
    scale = 1.0 / jnp.sqrt(ww)
    both = inverse * scale
    unit_w = lambda i, j: w[i, j] * both
    unit_q = lambda i, j: q[i, j] * both
    spread(2, 0, inner_products((unit_w, unit_q), (unit_q, unit_q), (scaled_v, unit_q)))
    for copy in arriving.values():
        copy.wait_send()
    for number in range(2):
        for phase in range(2):
            all_landed(number, phase).wait_send()
    spread(2, 1, gather(2, 0, 4)[:3])
    all_landed(2, 0).wait_send()
    wq, qq, bq = gather(2, 1, 3)
    wb = wb * scale
    second = (bq - wq * wb) / (qq - wq * wq)
    weight_1 = (wb - wq * second) * scale
    weight_2 = second * scale
    for i, j in NODES:
        out_ref[i, j] = weight_1 * c1[i, j] + weight_2 * c2[i, j]
    all_landed(2, 1).wait_send()


def solution(mesh):
    ngx, ngy = mesh.shape["gx"], mesh.shape["gy"]
    fast = 4
    others = 2 * (ngx // fast) - 1

    def local(load_vector, blocks):
        cx, cy, size, cases = load_vector.shape
        field = (cx, cy, size, cases)
        matrices = (cx, cy, size, size)
        sem = pltpu.SemaphoreType.DMA
        return pl.pallas_call(
            functools.partial(kernel, ngx, ngy, fast),
            out_shape=jax.ShapeDtypeStruct(field, F32),
            in_specs=[pl.BlockSpec(memory_space=pltpu.HBM)] * 2,
            out_specs=pl.BlockSpec(memory_space=pltpu.VMEM),
            scratch_shapes=[
                pltpu.VMEM(field, F32),
                pltpu.VMEM((4, *matrices), BF16),
                pltpu.VMEM(matrices, BF16),
                pltpu.VMEM(matrices, BF16),
                pltpu.VMEM((4, *field), BF16),
                pltpu.VMEM((4, 2, 2, size, cases), BF16),
                pltpu.VMEM((4, 4, 2, size, cases), BF16),
                pltpu.VMEM(field, F32),
                pltpu.VMEM(field, F32),
                pltpu.VMEM(field, F32),
                pltpu.VMEM(field, F32),
                pltpu.VMEM(field, F32),
                pltpu.VMEM(field, F32),
                *[pltpu.VMEM((2, terms, cases), F32) for terms in TERMS],
                *[pltpu.VMEM((2, others, terms, cases), F32) for terms in TERMS],
                sem((5,)),
                sem((4, 8)),
                sem((4, 8)),
                sem((len(TERMS), 2)),
                sem((len(TERMS), 2)),
            ],
            compiler_params=pltpu.CompilerParams(
                collective_id=0, has_side_effects=True, vmem_limit_bytes=48 * 1024 * 1024
            ),
        )(*[pltpu.with_memory_space_constraint(a, pltpu.HBM) for a in (load_vector, blocks)])

    return jax.shard_map(
        local,
        mesh=mesh,
        in_specs=(P("gx", "gy", None, None), P(None, "gx", "gy", None, None)),
        out_specs=P("gx", "gy", None, None),
        check_vma=False,
    )
```

```python
import functools

import jax
import jax.numpy as jnp
from jax import lax
from jax.experimental import pallas as pl
from jax.experimental.pallas import tpu as pltpu
from jax.sharding import PartitionSpec as P

MESH = pl.DeviceIdType.MESH
F32 = jnp.float32
BF16 = jnp.bfloat16
NODES = [(0, 0), (1, 0), (0, 1), (1, 1)]
XL, XH, YL, YH = range(4)
TERMS = (1, 4, 4)


def dot(a, b):
    return jnp.dot(a, b, preferred_element_type=F32)


def split(u):
    high = u.astype(BF16)
    return high, (u - high.astype(F32)).astype(BF16)


def dot2(a, u):
    both = dot(a, jnp.concatenate(split(u), axis=1))
    half = u.shape[1]
    return both[:, :half] + both[:, half:]


def shrink_of(square):
    return jnp.where(square > 0.0, jnp.minimum(1.0 / jnp.sqrt(square), 1e12), 1.0)


def extra_of(square):
    return jnp.where(square > 0.0, jnp.minimum(1.0 / jnp.sqrt(square), 1e12), 1e-8)


def over_rows(a):
    return jnp.sum(a, axis=0, keepdims=True)


def kernel(
    ngx, ngy, fast,
    load_ref, blocks_ref, out_ref,
    v, m, t1, t2, sent, products, halo, first, total, c1, c2, w, scaled_w, scaled_v,
    mine_0, mine_1, mine_2, landed_0, landed_1, landed_2,
    load_sem, halo_send, halo_recv, sum_send, sum_recv, circle,
):
    gx, gy = lax.axis_index("gx"), lax.axis_index("gy")
    up_x, down_x = lax.rem(gx + 1, ngx), lax.rem(gx + ngx - 1, ngx)
    up_y, down_y = lax.rem(gy + 1, ngy), lax.rem(gy + ngy - 1, ngy)
    sides = {XL: (up_x, gy), XH: (down_x, gy), YL: (gx, up_y), YH: (gx, down_y)}

    shape = (ngx // fast, fast, ngy // 2, 2)
    z, y, x, core = gx // fast, gx % fast, gy // 2, gy % 2

    def device(offset):
        dz, dy, dx, dc = offset
        return (
            lax.rem(z + dz, shape[0]) * fast + lax.rem(y + dy, shape[1]),
            lax.rem(x + dx, shape[2]) * 2 + lax.rem(core + dc, 2),
        )

    def offsets(*steps):
        wrapped = [tuple(d % n for d, n in zip(step, shape)) for step in steps]
        return [step for step in dict.fromkeys(wrapped) if any(step)]

    def hops(offset):
        return sum(min(d, n - d) for d, n in zip(offset, shape))

    ranges = [range(n) for n in shape]
    groups = [
        [device(step) for step in sorted(offsets(*steps), key=hops, reverse=True)]
        for steps in (
            [(dz, 0, 0, dc) for dz in ranges[0] for dc in ranges[3]],
            [(0, dy, dx, 0) for dy in ranges[1] for dx in ranges[2]],
        )
    ]
    near = [
        device(step)
        for step in offsets(
            (0, 0, 0, 1), (1, 0, 0, 0), (-1, 0, 0, 0), (1, 0, 0, 1), (-1, 0, 0, 1),
            (0, 1, 0, 0), (0, -1, 0, 0), (0, 0, 1, 0), (0, 0, -1, 0),
        )
    ]
    far = [device(step) for step in offsets((2, 0, 0, 0), (-2, 0, 0, 0), (0, 2, 0, 0), (0, 0, 2, 0))]
    mine = [mine_0, mine_1, mine_2]
    landed = [landed_0, landed_1, landed_2]

    barrier = pltpu.get_barrier_semaphore()
    partners = [*sides.values(), *near]
    for partner in partners:
        pl.semaphore_signal(barrier, inc=1, device_id=partner, device_id_type=MESH)

    loads = [
        pltpu.make_async_copy(load_ref, v, load_sem.at[0]),
        pltpu.make_async_copy(blocks_ref.at[3], m.at[3], load_sem.at[1]),
        pltpu.make_async_copy(blocks_ref.at[1], m.at[1], load_sem.at[2]),
        pltpu.make_async_copy(blocks_ref.at[2], m.at[2], load_sem.at[3]),
        pltpu.make_async_copy(blocks_ref.at[0], m.at[0], load_sem.at[4]),
    ]
    for copy in loads:
        copy.start()

    arriving = {}

    def send(source, step, side, place):
        slot = side * 2 + place
        copy = pltpu.make_async_remote_copy(
            src_ref=source,
            dst_ref=halo.at[step, side, place],
            send_sem=halo_send.at[step, slot],
            recv_sem=halo_recv.at[step, slot],
            device_id=sides[side],
            device_id_type=MESH,
        )
        copy.start()
        arriving[step, side, place] = copy

    def announce(step, i, j):
        if i == 0:
            send(sent.at[step, i, j], step, XH, j)
        if j == 0:
            send(sent.at[step, i, j], step, YH, i)

    def pass_up(step, i, j):
        if i == 1:
            products[step, 0, j] = dot(t1[1, j], sent[step, 1, j]).astype(BF16)
            send(products.at[step, 0, j], step, XL, j)
        if j == 1:
            products[step, 1, i] = dot(t2[i, 1], sent[step, i, 1]).astype(BF16)
            send(products.at[step, 1, i], step, YL, i)

    def exchange(step, field, compute):
        for i, j in NODES:
            value = compute(i, j)
            field[i, j] = value
            sent[step, i, j] = value.astype(BF16)
            announce(step, i, j)
            pass_up(step, i, j)

    def inner(step, field):
        for i, j in NODES:
            value = dot2(m[0, i, j], field[i, j]) if step < 3 else dot(m[0, i, j], sent[step, i, j])
            value += dot(m[1, 0, j], sent[step, 1, j]) if i == 0 else dot(t1[0, j], sent[step, 0, j])
            value += dot(m[2, i, 0], sent[step, i, 1]) if j == 0 else dot(t2[i, 0], sent[step, i, 0])
            total[i, j] = value

    def outer(step, i, j):
        value = total[i, j]
        if j == 0:
            arriving[step, YL, i].wait_recv()
            value += halo[step, YL, i].astype(F32)
        else:
            arriving[step, YH, i].wait_recv()
            value += dot(m[2, i, 1], halo[step, YH, i])
        if i == 0:
            arriving[step, XL, j].wait_recv()
            value += halo[step, XL, j].astype(F32)
        else:
            arriving[step, XH, j].wait_recv()
            value += dot(m[1, 1, j], halo[step, XH, j])
        return value

    def spread(number, phase, rows):
        for term, row in enumerate(rows):
            mine[number][phase, pl.ds(term, 1)] = row
        for slot, partner in enumerate(groups[phase]):
            pltpu.make_async_remote_copy(
                src_ref=mine[number].at[phase],
                dst_ref=landed[number].at[phase, slot],
                send_sem=sum_send.at[number, phase],
                recv_sem=sum_recv.at[number, phase],
                device_id=partner,
                device_id_type=MESH,
            ).start()

    def all_landed(number, phase):
        return pltpu.make_async_remote_copy(
            src_ref=landed[number].at[phase],
            dst_ref=landed[number].at[phase],
            send_sem=sum_send.at[number, phase],
            recv_sem=sum_recv.at[number, phase],
            device_id=groups[phase][0],
            device_id_type=MESH,
        )

    def gather(number, phase, count):
        all_landed(number, phase).wait_recv()
        value = mine[number][phase]
        for slot in range(len(groups[phase])):
            value += landed[number][phase, slot]
        return [value[term : term + 1] for term in range(count)]

    def inner_products(*pairs):
        rows = [None] * len(pairs)
        for i, j in NODES:
            for term, (a, b) in enumerate(pairs):
                part = over_rows(a[i, j] * b[i, j])
                rows[term] = part if rows[term] is None else rows[term] + part
        return rows

    mine_1[...] = jnp.zeros(mine_1.shape, F32)
    mine_2[...] = jnp.zeros(mine_2.shape, F32)

    loads[0].wait()
    loads[1].wait()
    for i, j in NODES:
        value = dot2(m[3, i, j], v[i, j])
        first[i, j] = value
        sent[0, i, j] = value.astype(BF16)
    pl.semaphore_wait(barrier, len(partners))
    for i, j in NODES:
        announce(0, i, j)
    for partner in near:
        pl.semaphore_signal(circle.at[0], inc=1, device_id=partner, device_id_type=MESH)
    loads[2].wait()
    loads[3].wait()

    @pl.when(gx == ngx - 1)
    def _():
        for j in range(2):
            m[1, 1, j] = jnp.zeros_like(m[1, 1, j])

    @pl.when(gy == ngy - 1)
    def _():
        for i in range(2):
            m[2, i, 1] = jnp.zeros_like(m[2, i, 1])

    for k in range(2):
        t1[1, k] = m[1, 1, k].T
    for k in range(2):
        t2[k, 1] = m[2, k, 1].T
    for i, j in NODES:
        pass_up(0, i, j)
    for k in range(2):
        t1[0, k] = m[1, 0, k].T
        t2[k, 0] = m[2, k, 0].T
    loads[4].wait()
    inner(0, first)
    pl.semaphore_wait(circle.at[0], len(near))
    for partner in far:
        pl.semaphore_signal(circle.at[1], inc=1, device_id=partner, device_id_type=MESH)

    exchange(1, c1, lambda i, j: first[i, j] + dot2(m[3, i, j], v[i, j] - outer(0, i, j)))
    pl.semaphore_wait(circle.at[1], len(far))
    spread(0, 0, inner_products((v, v)))
    inner(1, c1)

    def second_start(i, j):
        w[i, j] = outer(1, i, j)
        return dot2(m[3, i, j], w[i, j])

    exchange(2, first, second_start)
    (square,) = gather(0, 0, 1)
    shrink = shrink_of(square)
    for i, j in NODES:
        scaled_w[i, j] = w[i, j] * shrink
        scaled_v[i, j] = v[i, j] * shrink
    spread(1, 0, inner_products((scaled_w, scaled_w), (scaled_w, scaled_v)))
    inner(2, first)

    exchange(3, c2, lambda i, j: first[i, j] + dot2(m[3, i, j], w[i, j] - outer(2, i, j)))
    inner(3, c2)
    ww, wb = gather(1, 0, 2)
    extra = extra_of(ww)
    both = shrink * extra
    rows = [None] * 3
    for i, j in NODES:
        unit_q = outer(3, i, j) * both
        for term, other in enumerate((scaled_w[i, j], unit_q, scaled_v[i, j])):
            part = over_rows(other * unit_q)
            rows[term] = part if rows[term] is None else rows[term] + part
    spread(2, 0, rows)
    spread(1, 1, [square, ww, wb])
    for copy in arriving.values():
        copy.wait_send()
    all_landed(0, 0).wait_send()
    all_landed(1, 0).wait_send()
    spread(2, 1, gather(2, 0, 4)[:3])

    all_landed(1, 1).wait_recv()
    theirs = [(landed_1[1, slot, 0:1], landed_1[1, slot, 1:2], landed_1[1, slot, 2:3]) for slot in range(len(groups[1]))]
    theirs.append((square, ww, wb))
    norm_square = functools.reduce(jnp.add, [b for b, _, _ in theirs])
    inverse = 1.0 / jnp.sqrt(norm_square)
    ratios = [inverse / shrink_of(b) for b, _, _ in theirs]
    whole_ww = functools.reduce(jnp.add, [k * k * c for k, (_, c, _) in zip(ratios, theirs)])
    whole_wb = functools.reduce(jnp.add, [k * k * d for k, (_, _, d) in zip(ratios, theirs)])
    scale = 1.0 / jnp.sqrt(whole_ww)
    extras = [scale / extra_of(c) for _, c, _ in theirs]
    once = [k * k * e for k, e in zip(ratios, extras)]
    twice = [k * e for k, e in zip(once, extras)]
    all_landed(2, 0).wait_send()
    all_landed(1, 1).wait_send()

    all_landed(2, 1).wait_recv()
    last = [landed_2[1, slot] for slot in range(len(groups[1]))] + [mine_2[1]]
    wq = functools.reduce(jnp.add, [k * part[0:1] for k, part in zip(once, last)])
    qq = functools.reduce(jnp.add, [k * part[1:2] for k, part in zip(twice, last)])
    bq = functools.reduce(jnp.add, [k * part[2:3] for k, part in zip(once, last)])
    wq = wq * scale
    wb = whole_wb * scale
    second = (bq - wq * wb) / (qq - wq * wq)
    weight_1 = (wb - wq * second) * scale
    weight_2 = second * scale
    for i, j in NODES:
        out_ref[i, j] = weight_1 * c1[i, j] + weight_2 * c2[i, j]
    all_landed(2, 1).wait_send()


def solution(mesh):
    ngx, ngy = mesh.shape["gx"], mesh.shape["gy"]
    fast = 4
    others = 2 * (ngx // fast) - 1

    def local(load_vector, blocks):
        cx, cy, size, cases = load_vector.shape
        field = (cx, cy, size, cases)
        matrices = (cx, cy, size, size)
        sem = pltpu.SemaphoreType.DMA
        return pl.pallas_call(
            functools.partial(kernel, ngx, ngy, fast),
            out_shape=jax.ShapeDtypeStruct(field, F32),
            in_specs=[pl.BlockSpec(memory_space=pltpu.HBM)] * 2,
            out_specs=pl.BlockSpec(memory_space=pltpu.VMEM),
            scratch_shapes=[
                pltpu.VMEM(field, F32),
                pltpu.VMEM((4, *matrices), BF16),
                pltpu.VMEM(matrices, BF16),
                pltpu.VMEM(matrices, BF16),
                pltpu.VMEM((4, *field), BF16),
                pltpu.VMEM((4, 2, 2, size, cases), BF16),
                pltpu.VMEM((4, 4, 2, size, cases), BF16),
                pltpu.VMEM(field, F32),
                pltpu.VMEM(field, F32),
                pltpu.VMEM(field, F32),
                pltpu.VMEM(field, F32),
                pltpu.VMEM(field, F32),
                pltpu.VMEM(field, F32),
                pltpu.VMEM(field, F32),
                *[pltpu.VMEM((2, terms, cases), F32) for terms in TERMS],
                *[pltpu.VMEM((2, others, terms, cases), F32) for terms in TERMS],
                sem((5,)),
                sem((4, 8)),
                sem((4, 8)),
                sem((len(TERMS), 2)),
                sem((len(TERMS), 2)),
                pltpu.SemaphoreType.REGULAR((2,)),
            ],
            compiler_params=pltpu.CompilerParams(
                collective_id=0, has_side_effects=True, vmem_limit_bytes=48 * 1024 * 1024
            ),
        )(*[pltpu.with_memory_space_constraint(a, pltpu.HBM) for a in (load_vector, blocks)])

    return jax.shard_map(
        local,
        mesh=mesh,
        in_specs=(P("gx", "gy", None, None), P(None, "gx", "gy", None, None)),
        out_specs=P("gx", "gy", None, None),
        check_vma=False,
    )
```

```python
import functools

import jax
import jax.numpy as jnp
from jax import lax
from jax.experimental import pallas as pl
from jax.experimental.pallas import tpu as pltpu
from jax.sharding import PartitionSpec as P

MESH = pl.DeviceIdType.MESH
F32 = jnp.float32
BF16 = jnp.bfloat16
NODES = [(0, 0), (1, 0), (0, 1), (1, 1)]
EVEN, ODD = [(0, 0), (1, 0)], [(0, 1), (1, 1)]
PAIRS = [[[(0, 0)], [(1, 0)], [(0, 1)], [(1, 1)]]] * 5
XL, XH, YL, YH = range(4)
TERMS = (4, 4)


def dot(a, b):
    return jnp.dot(a, b, preferred_element_type=F32)


def split(u):
    high = u.astype(BF16)
    return high, (u - high.astype(F32)).astype(BF16)


def dot2(a, u):
    both = dot(a, jnp.concatenate(split(u), axis=1))
    half = u.shape[1]
    return both[:, :half] + both[:, half:]


def shrink_of(square):
    return jnp.where(square > 0.0, jnp.minimum(1.0 / jnp.sqrt(square), 1e12), 1.0)


def extra_of(square):
    return jnp.where(square > 0.0, jnp.minimum(1.0 / jnp.sqrt(square), 1e12), 1e-8)


def fold(a):
    return jnp.sum(a.reshape(-1, 8, a.shape[1]), axis=0)


def over_rows(a):
    return jnp.sum(a, axis=0, keepdims=True)


def kernel(
    ngx, ngy, fast,
    load_ref, blocks_ref, out_ref,
    v, m, t1, t2, reach, lift, up_base, sent, products, halo, first, total, c1, c2, w, scaled_w, scaled_v,
    mine_0, mine_1, landed_0, landed_1,
    load_sem, halo_send, halo_recv, sum_send, sum_recv, circle,
):
    gx, gy = lax.axis_index("gx"), lax.axis_index("gy")
    up_x, down_x = lax.rem(gx + 1, ngx), lax.rem(gx + ngx - 1, ngx)
    up_y, down_y = lax.rem(gy + 1, ngy), lax.rem(gy + ngy - 1, ngy)
    sides = {XL: (up_x, gy), XH: (down_x, gy), YL: (gx, up_y), YH: (gx, down_y)}
    has_up_x, has_down_x, has_up_y, has_down_y = gx < ngx - 1, gx > 0, gy < ngy - 1, gy > 0
    leaves = {XL: has_up_x, XH: has_down_x, YL: has_up_y, YH: has_down_y}
    arrives = {XL: has_down_x, XH: has_up_x, YL: has_down_y, YH: has_up_y}

    shape = (ngx // fast, fast, ngy // 2, 2)
    z, y, x, core = gx // fast, gx % fast, gy // 2, gy % 2
    chip = x

    def device(offset):
        dz, dy, dx, dc = offset
        return (
            lax.rem(z + dz, shape[0]) * fast + lax.rem(y + dy, shape[1]),
            lax.rem(x + dx, shape[2]) * 2 + lax.rem(core + dc, 2),
        )

    def offsets(*steps):
        wrapped = [tuple(d % n for d, n in zip(step, shape)) for step in steps]
        return [step for step in dict.fromkeys(wrapped) if any(step)]

    def hops(offset):
        return sum(min(d, n - d) for d, n in zip(offset, shape))

    ranges = [range(n) for n in shape]
    groups = [
        [device(step) for step in sorted(offsets(*steps), key=hops, reverse=True)]
        for steps in (
            [(dz, 0, 0, dc) for dz in ranges[0] for dc in ranges[3]],
            [(0, dy, dx, 0) for dy in ranges[1] for dx in ranges[2]],
        )
    ]
    def circle_of(*steps):
        wrapped = [(a % ngx, b % ngy) for a, b in steps]
        return [
            (lax.rem(gx + a, ngx), lax.rem(gy + b, ngy)) for a, b in dict.fromkeys(wrapped) if a or b
        ]

    circles = [
        circle_of((1, 0), (-1, 0), (0, 1), (0, -1)),
        circle_of((2, 0), (-2, 0), (0, 2), (0, -2)),
        circle_of((4, 0), (-4, 0), (0, 4)),
        circle_of((8, 0), (-8, 0)),
        [(gx, chip * 2 + 1 - core)],
    ]

    def tell(number):
        for partner in circles[number]:
            pl.semaphore_signal(circle.at[number], inc=1, device_id=partner, device_id_type=MESH)

    def hear(number):
        if circles[number]:
            pl.semaphore_wait(circle.at[number], len(circles[number]))

    mine = [mine_0, mine_1]
    landed = [landed_0, landed_1]

    barrier = pltpu.get_barrier_semaphore()
    for partner in sides.values():
        pl.semaphore_signal(barrier, inc=1, device_id=partner, device_id_type=MESH)

    loads = [
        pltpu.make_async_copy(load_ref, v, load_sem.at[0]),
        pltpu.make_async_copy(blocks_ref.at[3], m.at[3], load_sem.at[1]),
        pltpu.make_async_copy(blocks_ref.at[1], m.at[1], load_sem.at[2]),
        pltpu.make_async_copy(blocks_ref.at[2], m.at[2], load_sem.at[3]),
        pltpu.make_async_copy(blocks_ref.at[0], m.at[0], load_sem.at[4]),
    ]
    for copy in loads:
        copy.start()

    arriving = {}

    def send(source, step, side, place):
        slot = side * 2 + place
        copy = pltpu.make_async_remote_copy(
            src_ref=source,
            dst_ref=halo.at[step, side, place],
            send_sem=halo_send.at[step, slot],
            recv_sem=halo_recv.at[step, slot],
            device_id=sides[side],
            device_id_type=MESH,
        )
        pl.when(leaves[side])(copy.start)
        arriving[step, side, place] = copy

    def announce(step, i, j):
        if i == 0:
            send(sent.at[step, i, j], step, XH, j)
        if j == 0:
            send(sent.at[step, i, j], step, YH, i)

    def ups(pair):
        return [(0, j, 1, j) for i, j in pair if i == 1] + [(1, i, i, 1) for i, j in pair if j == 1]

    def upward(axis, i, j):
        return t2[i, j] if axis else t1[i, j]

    def pass_up(step, pair, values):
        for (axis, k, i, j), value in zip(ups(pair), values):
            products[step, axis, k] = value.astype(BF16)
        for axis, k, i, j in ups(pair):
            send(products.at[step, axis, k], step, YL if axis else XL, k)

    def reach_of(i, j):
        return [reach[0, j] if i else m[3, i, j], reach[1, i] if j else m[3, i, j]]

    def halos(step, i, j):
        return [halo[step, XH if i else XL, j], halo[step, YH if j else YL, i]]

    def through(matrices, step, i, j):
        across_x, across_y = halos(step, i, j)
        return dot(matrices[0], across_x) + dot(matrices[1], across_y)

    def prepare(field, base):
        for i, j in NODES:
            field[i, j] = base(i, j)
        for axis, k, i, j in ups(NODES):
            up_base[axis, k] = dot(upward(axis, i, j), field[i, j].astype(BF16))

    def exchange(step, field, sign):
        for pair in PAIRS[step]:
            for i, j in pair:
                land(step - 1, i, j)
            for i, j in pair:
                value = field[i, j] + sign * through(reach_of(i, j), step - 1, i, j)
                field[i, j] = value
                sent[step, i, j] = value.astype(BF16)
            values = [
                up_base[axis, k] + sign * through([lift[axis, 0, k], lift[axis, 1, k]], step - 1, i, j)
                for axis, k, i, j in ups(pair)
            ]
            for i, j in pair:
                announce(step, i, j)
            pass_up(step, pair, values)

    def inner(step, field):
        for i, j in NODES:
            value = dot2(m[0, i, j], field[i, j]) if step < 3 else dot(m[0, i, j], sent[step, i, j])
            value += dot(m[1, 0, j], sent[step, 1, j]) if i == 0 else dot(t1[0, j], sent[step, 0, j])
            value += dot(m[2, i, 0], sent[step, i, 1]) if j == 0 else dot(t2[i, 0], sent[step, i, 0])
            total[i, j] = value

    def land(step, i, j):
        for side, place in ((YH if j else YL, i), (XH if i else XL, j)):
            pl.when(arrives[side])(arriving[step, side, place].wait_recv)

    def outer(step, i, j):
        value = total[i, j]
        value += dot(m[2, i, 1], halo[step, YH, i]) if j else halo[step, YL, i].astype(F32)
        value += dot(m[1, 1, j], halo[step, XH, j]) if i else halo[step, XL, j].astype(F32)
        return value

    def spread(number, phase, rows):
        term = 0
        for row in rows:
            mine[number][phase, pl.ds(term, row.shape[0])] = row
            term += row.shape[0]
        for slot, partner in enumerate(groups[phase]):
            pltpu.make_async_remote_copy(
                src_ref=mine[number].at[phase],
                dst_ref=landed[number].at[phase, slot],
                send_sem=sum_send.at[number, phase],
                recv_sem=sum_recv.at[number, phase],
                device_id=partner,
                device_id_type=MESH,
            ).start()

    def all_landed(number, phase):
        return pltpu.make_async_remote_copy(
            src_ref=landed[number].at[phase],
            dst_ref=landed[number].at[phase],
            send_sem=sum_send.at[number, phase],
            recv_sem=sum_recv.at[number, phase],
            device_id=groups[phase][0],
            device_id_type=MESH,
        )

    def joined(parts, to=shrink_of):
        square = functools.reduce(jnp.add, [part[0:1] for part in parts])
        ratios = [to(square) / shrink_of(part[0:1]) for part in parts]
        others = [
            functools.reduce(jnp.add, [k * k * part[term : term + 1] for k, part in zip(ratios, parts)])
            for term in (1, 2)
        ]
        return [square, *others], ratios

    def inner_products(*pairs):
        rows = [None] * len(pairs)
        for i, j in NODES:
            for term, (a, b) in enumerate(pairs):
                part = fold(a[i, j] * b[i, j])
                rows[term] = part if rows[term] is None else rows[term] + part
        return [over_rows(row) for row in rows]

    for side in sides:

        @pl.when(jnp.logical_not(arrives[side]))
        def _():
            for step in range(4):
                halo[step, side] = jnp.zeros(halo.shape[2:], BF16)

    mine_0[...] = jnp.zeros(mine_0.shape, F32)
    mine_1[...] = jnp.zeros(mine_1.shape, F32)

    loads[0].wait()
    loads[1].wait()
    for i, j in NODES:
        value = dot2(m[3, i, j], v[i, j])
        first[i, j] = value
        sent[0, i, j] = value.astype(BF16)
    pl.semaphore_wait(barrier, len(sides))
    for i, j in EVEN + ODD:
        announce(0, i, j)
    tell(0)
    loads[2].wait()
    loads[3].wait()

    for k in range(2):
        t1[1, k] = m[1, 1, k].T
    for k in range(2):
        t2[k, 1] = m[2, k, 1].T
    pass_up(0, NODES, [dot(upward(axis, i, j), sent[0, i, j]) for axis, k, i, j in ups(NODES)])
    for k in range(2):
        t1[0, k] = m[1, 0, k].T
        t2[k, 0] = m[2, k, 0].T
    loads[4].wait()
    inner(0, first)
    for k in range(2):
        reach[0, k] = dot(m[3, 1, k], m[1, 1, k]).astype(BF16)
        reach[1, k] = dot(m[3, k, 1], m[2, k, 1]).astype(BF16)
    for axis, k, i, j in ups(NODES):
        for side, matrix in enumerate(reach_of(i, j)):
            lift[axis, side, k] = dot(upward(axis, i, j), matrix).astype(BF16)
    prepare(c1, lambda i, j: first[i, j] + dot2(m[3, i, j], v[i, j] - total[i, j]))
    hear(0)
    tell(1)

    exchange(1, c1, -1.0)
    hear(1)
    tell(2)
    inner(1, c1)
    prepare(first, lambda i, j: dot2(m[3, i, j], total[i, j]))
    (square,) = inner_products((v, v))
    shrink = shrink_of(square)
    for i, j in NODES:
        scaled_v[i, j] = v[i, j] * shrink
    hear(2)
    tell(3)

    exchange(2, first, 1.0)
    for i, j in NODES:
        w[i, j] = outer(1, i, j)
    inner(2, first)
    prepare(c2, lambda i, j: first[i, j] + dot2(m[3, i, j], w[i, j] - total[i, j]))
    for i, j in NODES:
        scaled_w[i, j] = w[i, j] * shrink
    sums = [square, *inner_products((scaled_w, scaled_w), (scaled_w, scaled_v))]
    hear(3)
    tell(4)
    hear(4)
    spread(0, 0, sums)

    exchange(3, c2, -1.0)
    inner(3, c2)
    all_landed(0, 0).wait_recv()
    group, ratios = joined([mine_0[0], *[landed_0[0, slot] for slot in range(len(groups[0]))]])
    square_of_group, ww, wb = group
    extra = extra_of(ww)
    whole_shrink = shrink_of(square_of_group)
    both = whole_shrink * extra
    ratio = whole_shrink / shrink
    rows = [None] * 3
    for i, j in EVEN + ODD:
        land(3, i, j)
        unit_q = outer(3, i, j) * both
        for term, other in enumerate((scaled_w[i, j], unit_q, scaled_v[i, j])):
            part = fold(other * unit_q)
            rows[term] = part if rows[term] is None else rows[term] + part
    rows = [over_rows(row) for row in rows]
    spread(1, 0, [rows[0] * ratio, rows[1], rows[2] * ratio])
    spread(0, 1, group)
    for (_, side, _), copy in arriving.items():
        pl.when(leaves[side])(copy.wait_send)
    all_landed(0, 0).wait_send()
    all_landed(1, 0).wait_recv()
    spread(1, 1, [functools.reduce(jnp.add, [mine_1[0], *[landed_1[0, slot] for slot in range(len(groups[0]))]])])

    all_landed(0, 1).wait_recv()
    theirs = [mine_0[1], *[landed_0[1, slot] for slot in range(len(groups[1]))]]
    (_, whole_ww, whole_wb), ratios = joined(theirs, lambda square: 1.0 / jnp.sqrt(square))
    scale = 1.0 / jnp.sqrt(whole_ww)
    extras = [scale / extra_of(part[1:2]) for part in theirs]
    once = [k * k * e for k, e in zip(ratios, extras)]
    twice = [k * e for k, e in zip(once, extras)]
    all_landed(1, 0).wait_send()
    all_landed(0, 1).wait_send()

    all_landed(1, 1).wait_recv()
    last = [mine_1[1], *[landed_1[1, slot] for slot in range(len(groups[1]))]]
    wq = functools.reduce(jnp.add, [k * part[0:1] for k, part in zip(once, last)])
    qq = functools.reduce(jnp.add, [k * part[1:2] for k, part in zip(twice, last)])
    bq = functools.reduce(jnp.add, [k * part[2:3] for k, part in zip(once, last)])
    wq = wq * scale
    wb = whole_wb * scale
    second = (bq - wq * wb) / (qq - wq * wq)
    weight_1 = (wb - wq * second) * scale
    weight_2 = second * scale
    for i, j in NODES:
        out_ref[i, j] = weight_1 * c1[i, j] + weight_2 * c2[i, j]
    all_landed(1, 1).wait_send()


def solution(mesh):
    ngx, ngy = mesh.shape["gx"], mesh.shape["gy"]
    fast = 4
    others = 2 * (ngx // fast) - 1

    def local(load_vector, blocks):
        cx, cy, size, cases = load_vector.shape
        field = (cx, cy, size, cases)
        matrices = (cx, cy, size, size)
        sem = pltpu.SemaphoreType.DMA
        return pl.pallas_call(
            functools.partial(kernel, ngx, ngy, fast),
            out_shape=jax.ShapeDtypeStruct(field, F32),
            in_specs=[pl.BlockSpec(memory_space=pltpu.HBM)] * 2,
            out_specs=pl.BlockSpec(memory_space=pltpu.VMEM),
            scratch_shapes=[
                pltpu.VMEM(field, F32),
                pltpu.VMEM((4, *matrices), BF16),
                pltpu.VMEM(matrices, BF16),
                pltpu.VMEM(matrices, BF16),
                pltpu.VMEM((2, 2, size, size), BF16),
                pltpu.VMEM((2, 2, 2, size, size), BF16),
                pltpu.VMEM((2, 2, size, cases), F32),
                pltpu.VMEM((4, *field), BF16),
                pltpu.VMEM((4, 2, 2, size, cases), BF16),
                pltpu.VMEM((4, 4, 2, size, cases), BF16),
                pltpu.VMEM(field, F32),
                pltpu.VMEM(field, F32),
                pltpu.VMEM(field, F32),
                pltpu.VMEM(field, F32),
                pltpu.VMEM(field, F32),
                pltpu.VMEM(field, F32),
                pltpu.VMEM(field, F32),
                *[pltpu.VMEM((2, terms, cases), F32) for terms in TERMS],
                *[pltpu.VMEM((2, others, terms, cases), F32) for terms in TERMS],
                sem((5,)),
                sem((4, 8)),
                sem((4, 8)),
                sem((len(TERMS), 2)),
                sem((len(TERMS), 2)),
                pltpu.SemaphoreType.REGULAR((5,)),
            ],
            compiler_params=pltpu.CompilerParams(
                collective_id=0, has_side_effects=True, vmem_limit_bytes=48 * 1024 * 1024
            ),
        )(*[pltpu.with_memory_space_constraint(a, pltpu.HBM) for a in (load_vector, blocks)])

    return jax.shard_map(
        local,
        mesh=mesh,
        in_specs=(P("gx", "gy", None, None), P(None, "gx", "gy", None, None)),
        out_specs=P("gx", "gy", None, None),
        check_vma=False,
    )
```

```python
import functools

import jax
import jax.numpy as jnp
from jax import lax
from jax.experimental import pallas as pl
from jax.experimental.pallas import tpu as pltpu
from jax.sharding import PartitionSpec as P

MESH = pl.DeviceIdType.MESH
F32 = jnp.float32
BF16 = jnp.bfloat16
NODES = [(0, 0), (1, 0), (0, 1), (1, 1)]
EVEN, ODD = [(0, 0), (1, 0)], [(0, 1), (1, 1)]
PAIRS = [[[(0, 0)], [(1, 0)], [(0, 1)], [(1, 1)]]] * 5
XL, XH, YL, YH = range(4)
TERMS = 4


def dot(a, b):
    return jnp.dot(a, b, preferred_element_type=F32)


def split(u):
    high = u.astype(BF16)
    return high, (u - high.astype(F32)).astype(BF16)


def dot2(a, u):
    both = dot(a, jnp.concatenate(split(u), axis=1))
    half = u.shape[1]
    return both[:, :half] + both[:, half:]


def shrink_of(square):
    return jnp.where(square > 0.0, jnp.minimum(1.0 / jnp.sqrt(square), 1e12), 1.0)


def extra_of(square):
    return jnp.where(square > 0.0, jnp.minimum(1.0 / jnp.sqrt(square), 1e12), 1e-8)


def fold(a):
    return jnp.sum(a.reshape(-1, 8, a.shape[1]), axis=0)


def over_rows(a):
    return jnp.sum(a, axis=0, keepdims=True)


def kernel(
    ngx, ngy, fast,
    load_ref, blocks_ref, out_ref,
    v, m, t1, t2, reach, lift, up_base, sent, products, halo, first, total, c1, c2, w, scaled_w, scaled_v,
    mine, landed,
    load_sem, halo_send, halo_recv, sum_send, sum_recv, circle,
):
    gx, gy = lax.axis_index("gx"), lax.axis_index("gy")
    up_x, down_x = lax.rem(gx + 1, ngx), lax.rem(gx + ngx - 1, ngx)
    up_y, down_y = lax.rem(gy + 1, ngy), lax.rem(gy + ngy - 1, ngy)
    sides = {XL: (up_x, gy), XH: (down_x, gy), YL: (gx, up_y), YH: (gx, down_y)}
    has_up_x, has_down_x, has_up_y, has_down_y = gx < ngx - 1, gx > 0, gy < ngy - 1, gy > 0
    leaves = {XL: has_up_x, XH: has_down_x, YL: has_up_y, YH: has_down_y}
    arrives = {XL: has_down_x, XH: has_up_x, YL: has_down_y, YH: has_up_y}

    shape = (ngx // fast, fast, ngy // 2, 2)
    z, y, x, core = gx // fast, gx % fast, gy // 2, gy % 2
    chip = x

    def device(offset):
        dz, dy, dx, dc = offset
        return (
            lax.rem(z + dz, shape[0]) * fast + lax.rem(y + dy, shape[1]),
            lax.rem(x + dx, shape[2]) * 2 + lax.rem(core + dc, 2),
        )

    def offsets(*steps):
        wrapped = [tuple(d % n for d, n in zip(step, shape)) for step in steps]
        return [step for step in dict.fromkeys(wrapped) if any(step)]

    def hops(offset):
        return sum(min(d, n - d) for d, n in zip(offset, shape))

    ranges = [range(n) for n in shape]
    groups = [
        [device(step) for step in sorted(offsets(*steps), key=hops, reverse=True)]
        for steps in (
            [(dz, 0, 0, dc) for dz in ranges[0] for dc in ranges[3]],
            [(0, dy, dx, 0) for dy in ranges[1] for dx in ranges[2]],
        )
    ]
    def circle_of(*steps):
        wrapped = [(a % ngx, b % ngy) for a, b in steps]
        return [
            (lax.rem(gx + a, ngx), lax.rem(gy + b, ngy)) for a, b in dict.fromkeys(wrapped) if a or b
        ]

    circles = [
        circle_of((1, 0), (-1, 0), (0, 1), (0, -1)),
        circle_of((2, 0), (-2, 0), (0, 2), (0, -2)),
        circle_of((4, 0), (-4, 0), (0, 4)),
        circle_of((8, 0), (-8, 0)),
        [(gx, chip * 2 + 1 - core)],
    ]

    def tell(number):
        for partner in circles[number]:
            pl.semaphore_signal(circle.at[number], inc=1, device_id=partner, device_id_type=MESH)

    def hear(number):
        if circles[number]:
            pl.semaphore_wait(circle.at[number], len(circles[number]))


    barrier = pltpu.get_barrier_semaphore()
    for partner in sides.values():
        pl.semaphore_signal(barrier, inc=1, device_id=partner, device_id_type=MESH)

    loads = [
        pltpu.make_async_copy(load_ref, v, load_sem.at[0]),
        pltpu.make_async_copy(blocks_ref.at[3], m.at[3], load_sem.at[1]),
        pltpu.make_async_copy(blocks_ref.at[1], m.at[1], load_sem.at[2]),
        pltpu.make_async_copy(blocks_ref.at[2], m.at[2], load_sem.at[3]),
        pltpu.make_async_copy(blocks_ref.at[0], m.at[0], load_sem.at[4]),
    ]
    for copy in loads:
        copy.start()

    arriving = {}

    def send(source, step, side, place):
        copy = pltpu.make_async_remote_copy(
            src_ref=source,
            dst_ref=halo.at[side, step, place],
            send_sem=halo_send.at[side],
            recv_sem=halo_recv.at[step % 2, side * 2 + place],
            device_id=sides[side],
            device_id_type=MESH,
        )
        pl.when(leaves[side])(copy.start)
        arriving[step, side, place] = copy

    def announce(step, i, j):
        if i == 0:
            send(sent.at[step, i, j], step, XH, j)
        if j == 0:
            send(sent.at[step, i, j], step, YH, i)

    def ups(pair):
        return [(0, j, 1, j) for i, j in pair if i == 1] + [(1, i, i, 1) for i, j in pair if j == 1]

    def upward(axis, i, j):
        return t2[i, j] if axis else t1[i, j]

    def pass_up(step, pair, values):
        for (axis, k, i, j), value in zip(ups(pair), values):
            products[step, axis, k] = value.astype(BF16)
        for axis, k, i, j in ups(pair):
            send(products.at[step, axis, k], step, YL if axis else XL, k)

    def reach_of(i, j):
        return [reach[0, j] if i else m[3, i, j], reach[1, i] if j else m[3, i, j]]

    def halos(step, i, j):
        return [halo[XH if i else XL, step, j], halo[YH if j else YL, step, i]]

    def through(matrices, step, i, j):
        across_x, across_y = halos(step, i, j)
        return dot(matrices[0], across_x) + dot(matrices[1], across_y)

    def prepare(field, base):
        for i, j in NODES:
            field[i, j] = base(i, j)
        for axis, k, i, j in ups(NODES):
            up_base[axis, k] = dot(upward(axis, i, j), field[i, j].astype(BF16))

    def exchange(step, field, sign):
        for pair in PAIRS[step]:
            for i, j in pair:
                land(step - 1, i, j)
            for i, j in pair:
                value = field[i, j] + sign * through(reach_of(i, j), step - 1, i, j)
                field[i, j] = value
                sent[step, i, j] = value.astype(BF16)
            values = [
                up_base[axis, k] + sign * through([lift[axis, 0, k], lift[axis, 1, k]], step - 1, i, j)
                for axis, k, i, j in ups(pair)
            ]
            for i, j in pair:
                announce(step, i, j)
            pass_up(step, pair, values)

    def inner(step, field):
        for i, j in NODES:
            value = dot2(m[0, i, j], field[i, j]) if step < 3 else dot(m[0, i, j], sent[step, i, j])
            value += dot(m[1, 0, j], sent[step, 1, j]) if i == 0 else dot(t1[0, j], sent[step, 0, j])
            value += dot(m[2, i, 0], sent[step, i, 1]) if j == 0 else dot(t2[i, 0], sent[step, i, 0])
            total[i, j] = value

    def land(step, i, j):
        for side, place in ((YH if j else YL, i), (XH if i else XL, j)):
            pl.when(arrives[side])(arriving[step, side, place].wait_recv)

    def outer(step, i, j):
        value = total[i, j]
        value += dot(m[2, i, 1], halo[YH, step, i]) if j else halo[YL, step, i].astype(F32)
        value += dot(m[1, 1, j], halo[XH, step, j]) if i else halo[XL, step, j].astype(F32)
        return value

    def spread(number, phase, rows):
        term = 0
        for row in rows:
            mine[number, phase, pl.ds(term, row.shape[0])] = row
            term += row.shape[0]
        for slot, partner in enumerate(groups[phase]):
            pltpu.make_async_remote_copy(
                src_ref=mine.at[number, phase],
                dst_ref=landed.at[number, phase, slot],
                send_sem=sum_send.at[0],
                recv_sem=sum_recv.at[number, phase],
                device_id=partner,
                device_id_type=MESH,
            ).start()

    def arrive(number, phase):
        pltpu.make_async_remote_copy(
            src_ref=landed.at[number, phase],
            dst_ref=landed.at[number, phase],
            send_sem=sum_send.at[0],
            recv_sem=sum_recv.at[number, phase],
            device_id=groups[phase][0],
            device_id_type=MESH,
        ).wait_recv()
        return [mine[number, phase], *[landed[number, phase, slot] for slot in range(len(groups[phase]))]]

    def joined(parts, to=shrink_of):
        square = functools.reduce(jnp.add, [part[0:1] for part in parts])
        ratios = [to(square) / shrink_of(part[0:1]) for part in parts]
        others = [
            functools.reduce(jnp.add, [k * k * part[term : term + 1] for k, part in zip(ratios, parts)])
            for term in (1, 2)
        ]
        return [square, *others], ratios

    def inner_products(*pairs):
        rows = [None] * len(pairs)
        for i, j in NODES:
            for term, (a, b) in enumerate(pairs):
                part = fold(a[i, j] * b[i, j])
                rows[term] = part if rows[term] is None else rows[term] + part
        return [over_rows(row) for row in rows]

    for side in sides:

        @pl.when(jnp.logical_not(arrives[side]))
        def _():
            halo[side] = jnp.zeros(halo.shape[1:], BF16)

    mine[...] = jnp.zeros(mine.shape, F32)

    loads[0].wait()
    loads[1].wait()
    for i, j in NODES:
        value = dot2(m[3, i, j], v[i, j])
        first[i, j] = value
        sent[0, i, j] = value.astype(BF16)
    pl.semaphore_wait(barrier, len(sides))
    for i, j in EVEN + ODD:
        announce(0, i, j)
    tell(0)
    loads[2].wait()
    loads[3].wait()

    for k in range(2):
        t1[1, k] = m[1, 1, k].T
    for k in range(2):
        t2[k, 1] = m[2, k, 1].T
    pass_up(0, NODES, [dot(upward(axis, i, j), sent[0, i, j]) for axis, k, i, j in ups(NODES)])
    for k in range(2):
        t1[0, k] = m[1, 0, k].T
        t2[k, 0] = m[2, k, 0].T
    loads[4].wait()
    inner(0, first)
    for k in range(2):
        reach[0, k] = dot(m[3, 1, k], m[1, 1, k]).astype(BF16)
        reach[1, k] = dot(m[3, k, 1], m[2, k, 1]).astype(BF16)
    for axis, k, i, j in ups(NODES):
        for side, matrix in enumerate(reach_of(i, j)):
            lift[axis, side, k] = dot(upward(axis, i, j), matrix).astype(BF16)
    prepare(c1, lambda i, j: first[i, j] + dot2(m[3, i, j], v[i, j] - total[i, j]))
    hear(0)
    tell(1)

    exchange(1, c1, -1.0)
    hear(1)
    tell(2)
    inner(1, c1)
    prepare(first, lambda i, j: dot2(m[3, i, j], total[i, j]))
    (square,) = inner_products((v, v))
    shrink = shrink_of(square)
    for i, j in NODES:
        scaled_v[i, j] = v[i, j] * shrink
    hear(2)
    tell(3)

    exchange(2, first, 1.0)
    for i, j in NODES:
        w[i, j] = outer(1, i, j)
    inner(2, first)
    prepare(c2, lambda i, j: first[i, j] + dot2(m[3, i, j], w[i, j] - total[i, j]))
    for i, j in NODES:
        scaled_w[i, j] = w[i, j] * shrink
    sums = [square, *inner_products((scaled_w, scaled_w), (scaled_w, scaled_v))]
    hear(3)
    tell(4)
    hear(4)
    spread(0, 0, sums)

    exchange(3, c2, -1.0)
    inner(3, c2)
    group, _ = joined(arrive(0, 0))
    square_of_group, ww, wb = group
    extra = extra_of(ww)
    whole_shrink = shrink_of(square_of_group)
    both = whole_shrink * extra
    ratio = whole_shrink / shrink
    rows = [None] * 3
    for i, j in EVEN + ODD:
        land(3, i, j)
        unit_q = outer(3, i, j) * both
        for term, other in enumerate((scaled_w[i, j], unit_q, scaled_v[i, j])):
            part = fold(other * unit_q)
            rows[term] = part if rows[term] is None else rows[term] + part
    rows = [over_rows(row) for row in rows]
    spread(1, 0, [rows[0] * ratio, rows[1], rows[2] * ratio])
    spread(0, 1, group)
    for side, partner in sides.items():
        all_sent = pltpu.make_async_remote_copy(
            src_ref=halo.at[side],
            dst_ref=halo.at[side],
            send_sem=halo_send.at[side],
            recv_sem=halo_recv.at[0, side],
            device_id=partner,
            device_id_type=MESH,
        )
        pl.when(leaves[side])(all_sent.wait_send)
    spread(1, 1, [functools.reduce(jnp.add, arrive(1, 0))])

    theirs = arrive(0, 1)
    (_, whole_ww, whole_wb), ratios = joined(theirs, lambda square: 1.0 / jnp.sqrt(square))
    scale = 1.0 / jnp.sqrt(whole_ww)
    extras = [scale / extra_of(part[1:2]) for part in theirs]
    once = [k * k * e for k, e in zip(ratios, extras)]
    twice = [k * e for k, e in zip(once, extras)]

    last = arrive(1, 1)
    wq = functools.reduce(jnp.add, [k * part[0:1] for k, part in zip(once, last)])
    qq = functools.reduce(jnp.add, [k * part[1:2] for k, part in zip(twice, last)])
    bq = functools.reduce(jnp.add, [k * part[2:3] for k, part in zip(once, last)])
    wq = wq * scale
    wb = whole_wb * scale
    second = (bq - wq * wb) / (qq - wq * wq)
    weight_1 = (wb - wq * second) * scale
    weight_2 = second * scale
    for i, j in NODES:
        out_ref[i, j] = weight_1 * c1[i, j] + weight_2 * c2[i, j]
    pltpu.make_async_remote_copy(
        src_ref=landed,
        dst_ref=landed,
        send_sem=sum_send.at[0],
        recv_sem=sum_recv.at[0, 0],
        device_id=groups[0][0],
        device_id_type=MESH,
    ).wait_send()


def solution(mesh):
    ngx, ngy = mesh.shape["gx"], mesh.shape["gy"]
    fast = 4
    others = 2 * (ngx // fast) - 1

    def local(load_vector, blocks):
        cx, cy, size, cases = load_vector.shape
        field = (cx, cy, size, cases)
        matrices = (cx, cy, size, size)
        sem = pltpu.SemaphoreType.DMA
        return pl.pallas_call(
            functools.partial(kernel, ngx, ngy, fast),
            out_shape=jax.ShapeDtypeStruct(field, F32),
            in_specs=[pl.BlockSpec(memory_space=pltpu.HBM)] * 2,
            out_specs=pl.BlockSpec(memory_space=pltpu.VMEM),
            scratch_shapes=[
                pltpu.VMEM(field, F32),
                pltpu.VMEM((4, *matrices), BF16),
                pltpu.VMEM(matrices, BF16),
                pltpu.VMEM(matrices, BF16),
                pltpu.VMEM((2, 2, size, size), BF16),
                pltpu.VMEM((2, 2, 2, size, size), BF16),
                pltpu.VMEM((2, 2, size, cases), F32),
                pltpu.VMEM((4, *field), BF16),
                pltpu.VMEM((4, 2, 2, size, cases), BF16),
                pltpu.VMEM((4, 4, 2, size, cases), BF16),
                pltpu.VMEM(field, F32),
                pltpu.VMEM(field, F32),
                pltpu.VMEM(field, F32),
                pltpu.VMEM(field, F32),
                pltpu.VMEM(field, F32),
                pltpu.VMEM(field, F32),
                pltpu.VMEM(field, F32),
                pltpu.VMEM((2, 2, TERMS, cases), F32),
                pltpu.VMEM((2, 2, others, TERMS, cases), F32),
                sem((5,)),
                sem((4,)),
                sem((2, 8)),
                sem((1,)),
                sem((2, 2)),
                pltpu.SemaphoreType.REGULAR((5,)),
            ],
            compiler_params=pltpu.CompilerParams(
                collective_id=0, has_side_effects=True, vmem_limit_bytes=48 * 1024 * 1024
            ),
        )(*[pltpu.with_memory_space_constraint(a, pltpu.HBM) for a in (load_vector, blocks)])

    return jax.shard_map(
        local,
        mesh=mesh,
        in_specs=(P("gx", "gy", None, None), P(None, "gx", "gy", None, None)),
        out_specs=P("gx", "gy", None, None),
        check_vma=False,
    )
```

```python
import functools

import jax
import jax.numpy as jnp
from jax import lax
from jax.experimental import pallas as pl
from jax.experimental.pallas import tpu as pltpu
from jax.sharding import PartitionSpec as P

MESH = pl.DeviceIdType.MESH
F32 = jnp.float32
BF16 = jnp.bfloat16
NODES = [(0, 0), (1, 0), (0, 1), (1, 1)]
EVEN, ODD = [(0, 0), (1, 0)], [(0, 1), (1, 1)]
PAIRS = [[[(0, 0)], [(1, 0)], [(0, 1)], [(1, 1)]]] * 5
XL, XH, YL, YH = range(4)
SLOTS = [(XL, 0), (XL, 1), (XH, 0), (XH, 1), (YL, None), (YH, None)]
TERMS = 4


def dot(a, b):
    return jnp.dot(a, b, preferred_element_type=F32)


def split(u):
    high = u.astype(BF16)
    return high, (u - high.astype(F32)).astype(BF16)


def dot2(a, u):
    both = dot(a, jnp.concatenate(split(u), axis=1))
    half = u.shape[1]
    return both[:, :half] + both[:, half:]


def shrink_of(square):
    return jnp.where(square > 0.0, jnp.minimum(1.0 / jnp.sqrt(square), 1e12), 1.0)


def extra_of(square):
    return jnp.where(square > 0.0, jnp.minimum(1.0 / jnp.sqrt(square), 1e12), 1e-8)


def fold(a):
    return jnp.sum(a.reshape(-1, 8, a.shape[1]), axis=0)


def over_rows(a):
    return jnp.sum(a, axis=0, keepdims=True)


def kernel(
    ngx, ngy, fast,
    load_ref, blocks_ref, out_ref,
    v, m, t1, t2, reach, lift, up_base, sent, products, halo, first, total, c1, c2, w, scaled_w, scaled_v,
    mine, landed,
    load_sem, halo_send, halo_recv, sum_send, sum_recv, circle,
):
    gx, gy = lax.axis_index("gx"), lax.axis_index("gy")
    up_x, down_x = lax.rem(gx + 1, ngx), lax.rem(gx + ngx - 1, ngx)
    up_y, down_y = lax.rem(gy + 1, ngy), lax.rem(gy + ngy - 1, ngy)
    sides = {XL: (up_x, gy), XH: (down_x, gy), YL: (gx, up_y), YH: (gx, down_y)}
    has_up_x, has_down_x, has_up_y, has_down_y = gx < ngx - 1, gx > 0, gy < ngy - 1, gy > 0
    leaves = {XL: has_up_x, XH: has_down_x, YL: has_up_y, YH: has_down_y}
    arrives = {XL: has_down_x, XH: has_up_x, YL: has_down_y, YH: has_up_y}

    shape = (ngx // fast, fast, ngy // 2, 2)
    z, y, x, core = gx // fast, gx % fast, gy // 2, gy % 2
    chip = x

    def device(offset):
        dz, dy, dx, dc = offset
        return (
            lax.rem(z + dz, shape[0]) * fast + lax.rem(y + dy, shape[1]),
            lax.rem(x + dx, shape[2]) * 2 + lax.rem(core + dc, 2),
        )

    def offsets(*steps):
        wrapped = [tuple(d % n for d, n in zip(step, shape)) for step in steps]
        return [step for step in dict.fromkeys(wrapped) if any(step)]

    ranges = [{8: (5, 4, 3, 2, 1, 6, 7, 0), 4: (1, 2, 3, 0), 2: (1, 0)}.get(n, range(n)) for n in shape]
    groups = [
        [device(step) for step in offsets(*steps)]
        for steps in (
            [(dz, 0, 0, dc) for dz in ranges[0] for dc in ranges[3]],
            [(0, dy, dx, 0) for dy in ranges[1] for dx in ranges[2]],
        )
    ]
    def circle_of(*steps):
        wrapped = [(a % ngx, b % ngy) for a, b in steps]
        return [
            (lax.rem(gx + a, ngx), lax.rem(gy + b, ngy)) for a, b in dict.fromkeys(wrapped) if a or b
        ]

    circles = [
        circle_of((1, 0), (-1, 0), (0, 1), (0, -1)),
        circle_of((2, 0), (-2, 0), (0, 2), (0, -2)),
        circle_of((4, 0), (-4, 0), (0, 4)),
        circle_of((8, 0), (-8, 0)),
        [(gx, chip * 2 + 1 - core)],
    ]

    def tell(number):
        for partner in circles[number]:
            pl.semaphore_signal(circle.at[number], inc=1, device_id=partner, device_id_type=MESH)

    def hear(number):
        if circles[number]:
            pl.semaphore_wait(circle.at[number], len(circles[number]))


    barrier = pltpu.get_barrier_semaphore()
    for partner in sides.values():
        pl.semaphore_signal(barrier, inc=1, device_id=partner, device_id_type=MESH)

    loads = [
        pltpu.make_async_copy(load_ref, v, load_sem.at[0]),
        pltpu.make_async_copy(blocks_ref.at[3], m.at[3], load_sem.at[1]),
        pltpu.make_async_copy(blocks_ref.at[pl.ds(1, 2)], m.at[pl.ds(1, 2)], load_sem.at[2]),
        pltpu.make_async_copy(blocks_ref.at[0], m.at[0], load_sem.at[3]),
    ]
    for copy in loads:
        copy.start()

    arriving = {}

    def send(source, step, side, place=None):
        target = halo.at[side, step] if place is None else halo.at[side, step, place]
        copy = pltpu.make_async_remote_copy(
            src_ref=source,
            dst_ref=target,
            send_sem=halo_send.at[side],
            recv_sem=halo_recv.at[step % 2, SLOTS.index((side, place))],
            device_id=sides[side],
            device_id_type=MESH,
        )
        pl.when(leaves[side])(copy.start)
        arriving[step, side, place] = copy

    def announce(step, i, j):
        if i == 0:
            send(sent.at[step, j, i], step, XH, j)
        if (i, j) == (1, 0):
            send(sent.at[step, j], step, YH)

    def ups(pair):
        return [(0, j, 1, j) for i, j in pair if i == 1] + [(1, i, i, 1) for i, j in pair if j == 1]

    def upward(axis, i, j):
        return t2[i, j] if axis else t1[i, j]

    def pass_up(step, pair, values):
        for (axis, k, i, j), value in zip(ups(pair), values):
            products[step, axis, k] = value.astype(BF16)
        for axis, k, i, j in ups(pair):
            if axis == 0:
                send(products.at[step, 0, k], step, XL, k)
            elif k == 1:
                send(products.at[step, 1], step, YL)

    def reach_of(i, j):
        return [reach[0, j] if i else m[3, i, j], reach[1, i] if j else m[3, i, j]]

    def halos(step, i, j):
        return [halo[XH if i else XL, step, j], halo[YH if j else YL, step, i]]

    def through(matrices, step, i, j):
        across_x, across_y = halos(step, i, j)
        return dot(matrices[0], across_x) + dot(matrices[1], across_y)

    def prepare(field, base):
        for i, j in NODES:
            field[i, j] = base(i, j)
        for axis, k, i, j in ups(NODES):
            up_base[axis, k] = dot(upward(axis, i, j), field[i, j].astype(BF16))

    def exchange(step, field, sign):
        for pair in PAIRS[step]:
            for i, j in pair:
                land(step - 1, i, j)
            for i, j in pair:
                value = field[i, j] + sign * through(reach_of(i, j), step - 1, i, j)
                field[i, j] = value
                sent[step, j, i] = value.astype(BF16)
            values = [
                up_base[axis, k] + sign * through([lift[axis, 0, k], lift[axis, 1, k]], step - 1, i, j)
                for axis, k, i, j in ups(pair)
            ]
            for i, j in pair:
                announce(step, i, j)
            pass_up(step, pair, values)

    def inner(step, field):
        for i, j in NODES:
            value = dot2(m[0, i, j], field[i, j]) if step < 3 else dot(m[0, i, j], sent[step, j, i])
            value += dot(m[1, 0, j], sent[step, j, 1]) if i == 0 else dot(t1[0, j], sent[step, j, 0])
            value += dot(m[2, i, 0], sent[step, 1, i]) if j == 0 else dot(t2[i, 0], sent[step, 0, i])
            total[i, j] = value

    def land(step, i, j):
        keys = [(XH if i else XL, j)]
        if i == 0:
            keys.append((YH if j else YL, None))
        for side, place in keys:
            pl.when(arrives[side])(arriving[step, side, place].wait_recv)

    def outer(step, i, j):
        value = total[i, j]
        value += dot(m[2, i, 1], halo[YH, step, i]) if j else halo[YL, step, i].astype(F32)
        value += dot(m[1, 1, j], halo[XH, step, j]) if i else halo[XL, step, j].astype(F32)
        return value

    def spread(number, phase, rows):
        term = 0
        for row in rows:
            mine[number, phase, pl.ds(term, row.shape[0])] = row
            term += row.shape[0]
        for slot, partner in enumerate(groups[phase]):
            pltpu.make_async_remote_copy(
                src_ref=mine.at[number, phase],
                dst_ref=landed.at[number, phase, slot],
                send_sem=sum_send.at[0],
                recv_sem=sum_recv.at[number, phase],
                device_id=partner,
                device_id_type=MESH,
            ).start()

    def arrive(number, phase):
        pltpu.make_async_remote_copy(
            src_ref=landed.at[number, phase],
            dst_ref=landed.at[number, phase],
            send_sem=sum_send.at[0],
            recv_sem=sum_recv.at[number, phase],
            device_id=groups[phase][0],
            device_id_type=MESH,
        ).wait_recv()
        return [mine[number, phase], *[landed[number, phase, slot] for slot in range(len(groups[phase]))]]

    def joined(parts, to=shrink_of):
        squares, sizes, overlaps = (
            jnp.concatenate([part[term : term + 1] for part in parts], axis=0) for term in range(3)
        )
        square = over_rows(squares)
        ratios = to(square) / shrink_of(squares)
        return [square, over_rows(ratios * ratios * sizes), over_rows(ratios * ratios * overlaps)], ratios, sizes

    def inner_products(*pairs):
        rows = [None] * len(pairs)
        for i, j in NODES:
            for term, (a, b) in enumerate(pairs):
                part = fold(a[i, j] * b[i, j])
                rows[term] = part if rows[term] is None else rows[term] + part
        return [over_rows(row) for row in rows]

    for side in sides:

        @pl.when(jnp.logical_not(arrives[side]))
        def _():
            halo[side] = jnp.zeros(halo.shape[1:], BF16)

    mine[...] = jnp.zeros(mine.shape, F32)

    loads[0].wait()
    loads[1].wait()
    for i, j in NODES:
        value = dot2(m[3, i, j], v[i, j])
        first[i, j] = value
        sent[0, j, i] = value.astype(BF16)
    pl.semaphore_wait(barrier, len(sides))
    for i, j in EVEN + ODD:
        announce(0, i, j)
    tell(0)
    loads[2].wait()

    for k in range(2):
        t1[1, k] = m[1, 1, k].T
    for k in range(2):
        t2[k, 1] = m[2, k, 1].T
    pass_up(0, NODES, [dot(upward(axis, i, j), sent[0, j, i]) for axis, k, i, j in ups(NODES)])
    for k in range(2):
        t1[0, k] = m[1, 0, k].T
        t2[k, 0] = m[2, k, 0].T
    loads[3].wait()
    inner(0, first)
    for k in range(2):
        reach[0, k] = dot(m[3, 1, k], m[1, 1, k]).astype(BF16)
        reach[1, k] = dot(m[3, k, 1], m[2, k, 1]).astype(BF16)
    for axis, k, i, j in ups(NODES):
        for side, matrix in enumerate(reach_of(i, j)):
            lift[axis, side, k] = dot(upward(axis, i, j), matrix).astype(BF16)
    prepare(c1, lambda i, j: first[i, j] + dot2(m[3, i, j], v[i, j] - total[i, j]))
    hear(0)
    tell(1)

    exchange(1, c1, -1.0)
    hear(1)
    tell(2)
    inner(1, c1)
    prepare(first, lambda i, j: dot2(m[3, i, j], total[i, j]))
    (square,) = inner_products((v, v))
    shrink = shrink_of(square)
    for i, j in NODES:
        scaled_v[i, j] = v[i, j] * shrink
    hear(2)
    tell(3)

    exchange(2, first, 1.0)
    for i, j in NODES:
        w[i, j] = outer(1, i, j)
    inner(2, first)
    prepare(c2, lambda i, j: first[i, j] + dot2(m[3, i, j], w[i, j] - total[i, j]))
    for i, j in NODES:
        scaled_w[i, j] = w[i, j] * shrink
    sums = [square, *inner_products((scaled_w, scaled_w), (scaled_w, scaled_v))]
    hear(3)
    tell(4)
    hear(4)
    spread(0, 0, sums)

    exchange(3, c2, -1.0)
    inner(3, c2)
    group, _, _ = joined(arrive(0, 0))
    square_of_group, ww, wb = group
    extra = extra_of(ww)
    whole_shrink = shrink_of(square_of_group)
    both = whole_shrink * extra
    ratio = whole_shrink / shrink
    rows = [None] * 3
    for i, j in EVEN + ODD:
        land(3, i, j)
        unit_q = outer(3, i, j) * both
        for term, other in enumerate((scaled_w[i, j], unit_q, scaled_v[i, j])):
            part = fold(other * unit_q)
            rows[term] = part if rows[term] is None else rows[term] + part
    rows = [over_rows(row) for row in rows]
    spread(1, 0, [rows[0] * ratio, rows[1], rows[2] * ratio])
    spread(0, 1, group)
    for side, partner in sides.items():
        all_sent = pltpu.make_async_remote_copy(
            src_ref=halo.at[side],
            dst_ref=halo.at[side],
            send_sem=halo_send.at[side],
            recv_sem=halo_recv.at[0, side],
            device_id=partner,
            device_id_type=MESH,
        )
        pl.when(leaves[side])(all_sent.wait_send)
    spread(1, 1, [functools.reduce(jnp.add, arrive(1, 0))])

    theirs = arrive(0, 1)
    (_, whole_ww, whole_wb), ratios, sizes = joined(theirs, lambda square: 1.0 / jnp.sqrt(square))
    scale = 1.0 / jnp.sqrt(whole_ww)
    extras = scale / extra_of(sizes)
    once = ratios * ratios * extras
    twice = once * extras
    factors = []
    for k in range(len(theirs)):
        row = once[k : k + 1]
        factors.append(jnp.concatenate([row, twice[k : k + 1], row, row], axis=0))

    last = functools.reduce(jnp.add, [factor * part for factor, part in zip(factors, arrive(1, 1))])
    wq, qq, bq = last[0:1], last[1:2], last[2:3]
    wq = wq * scale
    wb = whole_wb * scale
    second = (bq - wq * wb) / (qq - wq * wq)
    weight_1 = (wb - wq * second) * scale
    weight_2 = second * scale
    for i, j in NODES:
        out_ref[i, j] = weight_1 * c1[i, j] + weight_2 * c2[i, j]
    pltpu.make_async_remote_copy(
        src_ref=landed,
        dst_ref=landed,
        send_sem=sum_send.at[0],
        recv_sem=sum_recv.at[0, 0],
        device_id=groups[0][0],
        device_id_type=MESH,
    ).wait_send()


def solution(mesh):
    ngx, ngy = mesh.shape["gx"], mesh.shape["gy"]
    fast = 4
    others = 2 * (ngx // fast) - 1

    def local(load_vector, blocks):
        cx, cy, size, cases = load_vector.shape
        field = (cx, cy, size, cases)
        matrices = (cx, cy, size, size)
        sem = pltpu.SemaphoreType.DMA
        return pl.pallas_call(
            functools.partial(kernel, ngx, ngy, fast),
            out_shape=jax.ShapeDtypeStruct(field, F32),
            in_specs=[pl.BlockSpec(memory_space=pltpu.HBM)] * 2,
            out_specs=pl.BlockSpec(memory_space=pltpu.VMEM),
            scratch_shapes=[
                pltpu.VMEM(field, F32),
                pltpu.VMEM((4, *matrices), BF16),
                pltpu.VMEM(matrices, BF16),
                pltpu.VMEM(matrices, BF16),
                pltpu.VMEM((2, 2, size, size), BF16),
                pltpu.VMEM((2, 2, 2, size, size), BF16),
                pltpu.VMEM((2, 2, size, cases), F32),
                pltpu.VMEM((4, *field), BF16),
                pltpu.VMEM((4, 2, 2, size, cases), BF16),
                pltpu.VMEM((4, 4, 2, size, cases), BF16),
                pltpu.VMEM(field, F32),
                pltpu.VMEM(field, F32),
                pltpu.VMEM(field, F32),
                pltpu.VMEM(field, F32),
                pltpu.VMEM(field, F32),
                pltpu.VMEM(field, F32),
                pltpu.VMEM(field, F32),
                pltpu.VMEM((2, 2, TERMS, cases), F32),
                pltpu.VMEM((2, 2, others, TERMS, cases), F32),
                sem((4,)),
                sem((4,)),
                sem((2, len(SLOTS))),
                sem((1,)),
                sem((2, 2)),
                pltpu.SemaphoreType.REGULAR((5,)),
            ],
            compiler_params=pltpu.CompilerParams(
                collective_id=0, has_side_effects=True, vmem_limit_bytes=48 * 1024 * 1024
            ),
        )(*[pltpu.with_memory_space_constraint(a, pltpu.HBM) for a in (load_vector, blocks)])

    return jax.shard_map(
        local,
        mesh=mesh,
        in_specs=(P("gx", "gy", None, None), P(None, "gx", "gy", None, None)),
        out_specs=P("gx", "gy", None, None),
        check_vma=False,
    )
```

```python
import functools

import jax
import jax.numpy as jnp
from jax import lax
from jax.experimental import pallas as pl
from jax.experimental.pallas import tpu as pltpu
from jax.sharding import PartitionSpec as P

MESH = pl.DeviceIdType.MESH
F32 = jnp.float32
BF16 = jnp.bfloat16
NODES = [(0, 0), (1, 0), (0, 1), (1, 1)]
XL, XH, YL, YH = range(4)
SLOTS = [(XL, 0), (XL, 1), (XH, 0), (XH, 1), (YL, None), (YH, None)]
TERMS = 4


def dot(a, b):
    return jnp.dot(a, b, preferred_element_type=F32)


def split(u):
    high = u.astype(BF16)
    return high, (u - high.astype(F32)).astype(BF16)


def dot2(a, u):
    both = dot(a, jnp.concatenate(split(u), axis=1))
    half = u.shape[1]
    return both[:, :half] + both[:, half:]


def shrink_of(square):
    return jnp.where(square > 0.0, jnp.minimum(1.0 / jnp.sqrt(square), 1e12), 1.0)


def extra_of(square):
    return jnp.where(square > 0.0, jnp.minimum(1.0 / jnp.sqrt(square), 1e12), 1e-8)


def fold(a):
    return jnp.sum(a.reshape(-1, 8, a.shape[1]), axis=0)


def over_rows(a):
    return jnp.sum(a, axis=0, keepdims=True)


def kernel(
    ngx, ngy, fast,
    load_ref, blocks_ref, out_ref,
    v, m, t1, t2, reach, lift, up_base, sent, products, halo, first, total, c1, c2, w, scaled_w, scaled_v,
    mine, landed,
    load_sem, halo_send, halo_recv, sum_send, sum_recv, circle,
):
    gx, gy = lax.axis_index("gx"), lax.axis_index("gy")
    up_x, down_x = lax.rem(gx + 1, ngx), lax.rem(gx + ngx - 1, ngx)
    up_y, down_y = lax.rem(gy + 1, ngy), lax.rem(gy + ngy - 1, ngy)
    sides = {XL: (up_x, gy), XH: (down_x, gy), YL: (gx, up_y), YH: (gx, down_y)}
    has_up_x, has_down_x, has_up_y, has_down_y = gx < ngx - 1, gx > 0, gy < ngy - 1, gy > 0
    leaves = {XL: has_up_x, XH: has_down_x, YL: has_up_y, YH: has_down_y}
    arrives = {XL: has_down_x, XH: has_up_x, YL: has_down_y, YH: has_up_y}

    shape = (ngx // fast, fast, ngy // 2, 2)
    z, y, x, core = gx // fast, gx % fast, gy // 2, gy % 2

    def device(offset):
        dz, dy, dx, dc = offset
        return (
            lax.rem(z + dz, shape[0]) * fast + lax.rem(y + dy, shape[1]),
            lax.rem(x + dx, shape[2]) * 2 + lax.rem(core + dc, 2),
        )

    def offsets(*steps):
        wrapped = [tuple(d % n for d, n in zip(step, shape)) for step in steps]
        return [step for step in dict.fromkeys(wrapped) if any(step)]

    ranges = [{8: (5, 4, 3, 2, 1, 6, 7, 0), 4: (1, 2, 3, 0), 2: (1, 0)}.get(n, range(n)) for n in shape]
    groups = [
        [device(step) for step in offsets(*steps)]
        for steps in (
            [(dz, 0, 0, dc) for dz in ranges[0] for dc in ranges[3]],
            [(0, dy, dx, 0) for dy in ranges[1] for dx in ranges[2]],
        )
    ]
    def circle_of(*steps):
        wrapped = [(a % ngx, b % ngy) for a, b in steps]
        return [
            (lax.rem(gx + a, ngx), lax.rem(gy + b, ngy)) for a, b in dict.fromkeys(wrapped) if a or b
        ]

    circles = [
        circle_of((1, 0), (-1, 0), (0, 1), (0, -1)),
        circle_of((2, 0), (-2, 0), (0, 2), (0, -2)),
        circle_of((4, 0), (-4, 0), (0, 4)),
        circle_of((8, 0), (-8, 0)),
        [(gx, x * 2 + 1 - core)],
    ]

    def tell(number):
        for partner in circles[number]:
            pl.semaphore_signal(circle.at[number], inc=1, device_id=partner, device_id_type=MESH)

    def hear(number):
        if circles[number]:
            pl.semaphore_wait(circle.at[number], len(circles[number]))


    barrier = pltpu.get_barrier_semaphore()
    for partner in sides.values():
        pl.semaphore_signal(barrier, inc=1, device_id=partner, device_id_type=MESH)

    loads = [
        pltpu.make_async_copy(load_ref, v, load_sem.at[0]),
        pltpu.make_async_copy(blocks_ref.at[3], m.at[3], load_sem.at[1]),
        pltpu.make_async_copy(blocks_ref.at[pl.ds(1, 2)], m.at[pl.ds(1, 2)], load_sem.at[2]),
        pltpu.make_async_copy(blocks_ref.at[0], m.at[0], load_sem.at[3]),
    ]
    for copy in loads:
        copy.start()

    arriving = {}

    def send(source, step, side, place=None):
        target = halo.at[side, step] if place is None else halo.at[side, step, place]
        copy = pltpu.make_async_remote_copy(
            src_ref=source,
            dst_ref=target,
            send_sem=halo_send.at[side],
            recv_sem=halo_recv.at[step % 2, SLOTS.index((side, place))],
            device_id=sides[side],
            device_id_type=MESH,
        )
        pl.when(leaves[side])(copy.start)
        arriving[step, side, place] = copy

    def announce(step, i, j):
        if i == 0:
            send(sent.at[step, j, i], step, XH, j)
        if (i, j) == (1, 0):
            send(sent.at[step, j], step, YH)

    def ups(pair):
        return [(0, j, 1, j) for i, j in pair if i == 1] + [(1, i, i, 1) for i, j in pair if j == 1]

    def upward(axis, i, j):
        return t2[i, j] if axis else t1[i, j]

    def pass_up(step, pair, values):
        for (axis, k, i, j), value in zip(ups(pair), values):
            products[step, axis, k] = value.astype(BF16)
        for axis, k, i, j in ups(pair):
            if axis == 0:
                send(products.at[step, 0, k], step, XL, k)
            elif k == 1:
                send(products.at[step, 1], step, YL)

    def reach_of(i, j):
        return [reach[0, j] if i else m[3, i, j], reach[1, i] if j else m[3, i, j]]

    def halos(step, i, j):
        return [halo[XH if i else XL, step, j], halo[YH if j else YL, step, i]]

    def through(matrices, step, i, j):
        across_x, across_y = halos(step, i, j)
        return dot(matrices[0], across_x) + dot(matrices[1], across_y)

    def prepare(field, base):
        for i, j in NODES:
            field[i, j] = base(i, j)
        for axis, k, i, j in ups(NODES):
            up_base[axis, k] = dot(upward(axis, i, j), field[i, j].astype(BF16))

    def exchange(step, field, sign):
        for i, j in NODES:
            land(step - 1, i, j)
            value = field[i, j] + sign * through(reach_of(i, j), step - 1, i, j)
            field[i, j] = value
            sent[step, j, i] = value.astype(BF16)
            values = [
                up_base[axis, k] + sign * through([lift[axis, 0, k], lift[axis, 1, k]], step - 1, i, j)
                for axis, k, i, j in ups([(i, j)])
            ]
            announce(step, i, j)
            pass_up(step, [(i, j)], values)

    def inner(step, field):
        for i, j in NODES:
            value = dot2(m[0, i, j], field[i, j]) if step < 3 else dot(m[0, i, j], sent[step, j, i])
            value += dot(m[1, 0, j], sent[step, j, 1]) if i == 0 else dot(t1[0, j], sent[step, j, 0])
            value += dot(m[2, i, 0], sent[step, 1, i]) if j == 0 else dot(t2[i, 0], sent[step, 0, i])
            total[i, j] = value

    def land(step, i, j):
        keys = [(XH if i else XL, j)]
        if i == 0:
            keys.append((YH if j else YL, None))
        for side, place in keys:
            pl.when(arrives[side])(arriving[step, side, place].wait_recv)

    def outer(step, i, j):
        value = total[i, j]
        value += dot(m[2, i, 1], halo[YH, step, i]) if j else halo[YL, step, i].astype(F32)
        value += dot(m[1, 1, j], halo[XH, step, j]) if i else halo[XL, step, j].astype(F32)
        return value

    def spread(number, phase, rows):
        term = 0
        for row in rows:
            mine[number, phase, pl.ds(term, row.shape[0])] = row
            term += row.shape[0]
        for slot, partner in enumerate(groups[phase]):
            pltpu.make_async_remote_copy(
                src_ref=mine.at[number, phase],
                dst_ref=landed.at[number, phase, slot],
                send_sem=sum_send.at[0],
                recv_sem=sum_recv.at[number, phase],
                device_id=partner,
                device_id_type=MESH,
            ).start()

    def arrive(number, phase):
        pltpu.make_async_remote_copy(
            src_ref=landed.at[number, phase],
            dst_ref=landed.at[number, phase],
            send_sem=sum_send.at[0],
            recv_sem=sum_recv.at[number, phase],
            device_id=groups[phase][0],
            device_id_type=MESH,
        ).wait_recv()
        return [mine[number, phase], *[landed[number, phase, slot] for slot in range(len(groups[phase]))]]

    def joined(parts, to=shrink_of):
        squares, sizes, overlaps = (
            jnp.concatenate([part[term : term + 1] for part in parts], axis=0) for term in range(3)
        )
        square = over_rows(squares)
        ratios = to(square) / shrink_of(squares)
        return [square, over_rows(ratios * ratios * sizes), over_rows(ratios * ratios * overlaps)], ratios, sizes

    def inner_products(*pairs):
        rows = [None] * len(pairs)
        for i, j in NODES:
            for term, (a, b) in enumerate(pairs):
                part = fold(a[i, j] * b[i, j])
                rows[term] = part if rows[term] is None else rows[term] + part
        return [over_rows(row) for row in rows]

    for side in sides:

        @pl.when(jnp.logical_not(arrives[side]))
        def _():
            halo[side] = jnp.zeros(halo.shape[1:], BF16)

    mine[...] = jnp.zeros(mine.shape, F32)

    loads[0].wait()
    loads[1].wait()
    for i, j in NODES:
        value = dot2(m[3, i, j], v[i, j])
        first[i, j] = value
        sent[0, j, i] = value.astype(BF16)
    pl.semaphore_wait(barrier, len(sides))
    for i, j in NODES:
        announce(0, i, j)
    tell(0)
    loads[2].wait()

    for k in range(2):
        t1[1, k] = m[1, 1, k].T
    for k in range(2):
        t2[k, 1] = m[2, k, 1].T
    pass_up(0, NODES, [dot(upward(axis, i, j), sent[0, j, i]) for axis, k, i, j in ups(NODES)])
    for k in range(2):
        t1[0, k] = m[1, 0, k].T
        t2[k, 0] = m[2, k, 0].T
    loads[3].wait()
    inner(0, first)
    for k in range(2):
        reach[0, k] = dot(m[3, 1, k], m[1, 1, k]).astype(BF16)
        reach[1, k] = dot(m[3, k, 1], m[2, k, 1]).astype(BF16)
    for axis, k, i, j in ups(NODES):
        for side, matrix in enumerate(reach_of(i, j)):
            lift[axis, side, k] = dot(upward(axis, i, j), matrix).astype(BF16)
    prepare(c1, lambda i, j: first[i, j] + dot2(m[3, i, j], v[i, j] - total[i, j]))
    hear(0)
    tell(1)

    exchange(1, c1, -1.0)
    hear(1)
    tell(2)
    inner(1, c1)
    prepare(first, lambda i, j: dot2(m[3, i, j], total[i, j]))
    (square,) = inner_products((v, v))
    shrink = shrink_of(square)
    for i, j in NODES:
        scaled_v[i, j] = v[i, j] * shrink
    hear(2)
    tell(3)

    exchange(2, first, 1.0)
    for i, j in NODES:
        w[i, j] = outer(1, i, j)
    inner(2, first)
    prepare(c2, lambda i, j: first[i, j] + dot2(m[3, i, j], w[i, j] - total[i, j]))
    for i, j in NODES:
        scaled_w[i, j] = w[i, j] * shrink
    sums = [square, *inner_products((scaled_w, scaled_w), (scaled_w, scaled_v))]
    hear(3)
    tell(4)
    hear(4)
    spread(0, 0, sums)

    exchange(3, c2, -1.0)
    inner(3, c2)
    group, _, _ = joined(arrive(0, 0))
    square_of_group, ww, wb = group
    extra = extra_of(ww)
    whole_shrink = shrink_of(square_of_group)
    both = whole_shrink * extra
    ratio = whole_shrink / shrink
    rows = [None] * 3
    for i, j in NODES:
        land(3, i, j)
        unit_q = outer(3, i, j) * both
        for term, other in enumerate((scaled_w[i, j], unit_q, scaled_v[i, j])):
            part = fold(other * unit_q)
            rows[term] = part if rows[term] is None else rows[term] + part
    rows = [over_rows(row) for row in rows]
    spread(1, 0, [rows[0] * ratio, rows[1], rows[2] * ratio])
    spread(0, 1, group)
    for side, partner in sides.items():
        all_sent = pltpu.make_async_remote_copy(
            src_ref=halo.at[side],
            dst_ref=halo.at[side],
            send_sem=halo_send.at[side],
            recv_sem=halo_recv.at[0, side],
            device_id=partner,
            device_id_type=MESH,
        )
        pl.when(leaves[side])(all_sent.wait_send)
    spread(1, 1, [functools.reduce(jnp.add, arrive(1, 0))])

    theirs = arrive(0, 1)
    (_, whole_ww, whole_wb), ratios, sizes = joined(theirs, lambda square: 1.0 / jnp.sqrt(square))
    scale = 1.0 / jnp.sqrt(whole_ww)
    extras = scale / extra_of(sizes)
    once = ratios * ratios * extras
    twice = once * extras
    factors = []
    for k in range(len(theirs)):
        row = once[k : k + 1]
        factors.append(jnp.concatenate([row, twice[k : k + 1], row, row], axis=0))

    last = functools.reduce(jnp.add, [factor * part for factor, part in zip(factors, arrive(1, 1))])
    wq, qq, bq = last[0:1], last[1:2], last[2:3]
    wq = wq * scale
    wb = whole_wb * scale
    second = (bq - wq * wb) / (qq - wq * wq)
    weight_1 = (wb - wq * second) * scale
    weight_2 = second * scale
    for i, j in NODES:
        out_ref[i, j] = weight_1 * c1[i, j] + weight_2 * c2[i, j]
    pltpu.make_async_remote_copy(
        src_ref=landed,
        dst_ref=landed,
        send_sem=sum_send.at[0],
        recv_sem=sum_recv.at[0, 0],
        device_id=groups[0][0],
        device_id_type=MESH,
    ).wait_send()


def solution(mesh):
    ngx, ngy = mesh.shape["gx"], mesh.shape["gy"]
    fast = 4
    others = 2 * (ngx // fast) - 1

    def local(load_vector, blocks):
        cx, cy, size, cases = load_vector.shape
        field = (cx, cy, size, cases)
        matrices = (cx, cy, size, size)
        sem = pltpu.SemaphoreType.DMA
        return pl.pallas_call(
            functools.partial(kernel, ngx, ngy, fast),
            out_shape=jax.ShapeDtypeStruct(field, F32),
            in_specs=[pl.BlockSpec(memory_space=pltpu.HBM)] * 2,
            out_specs=pl.BlockSpec(memory_space=pltpu.VMEM),
            scratch_shapes=[
                pltpu.VMEM(field, F32),
                pltpu.VMEM((4, *matrices), BF16),
                pltpu.VMEM(matrices, BF16),
                pltpu.VMEM(matrices, BF16),
                pltpu.VMEM((2, 2, size, size), BF16),
                pltpu.VMEM((2, 2, 2, size, size), BF16),
                pltpu.VMEM((2, 2, size, cases), F32),
                pltpu.VMEM((4, *field), BF16),
                pltpu.VMEM((4, 2, 2, size, cases), BF16),
                pltpu.VMEM((4, 4, 2, size, cases), BF16),
                pltpu.VMEM(field, F32),
                pltpu.VMEM(field, F32),
                pltpu.VMEM(field, F32),
                pltpu.VMEM(field, F32),
                pltpu.VMEM(field, F32),
                pltpu.VMEM(field, F32),
                pltpu.VMEM(field, F32),
                pltpu.VMEM((2, 2, TERMS, cases), F32),
                pltpu.VMEM((2, 2, others, TERMS, cases), F32),
                sem((4,)),
                sem((4,)),
                sem((2, len(SLOTS))),
                sem((1,)),
                sem((2, 2)),
                pltpu.SemaphoreType.REGULAR((5,)),
            ],
            compiler_params=pltpu.CompilerParams(
                collective_id=0, has_side_effects=True, vmem_limit_bytes=48 * 1024 * 1024
            ),
        )(*[pltpu.with_memory_space_constraint(a, pltpu.HBM) for a in (load_vector, blocks)])

    return jax.shard_map(
        local,
        mesh=mesh,
        in_specs=(P("gx", "gy", None, None), P(None, "gx", "gy", None, None)),
        out_specs=P("gx", "gy", None, None),
        check_vma=False,
    )
```

```python
import functools

import jax
import jax.numpy as jnp
from jax import lax
from jax.experimental import pallas as pl
from jax.experimental.pallas import tpu as pltpu
from jax.sharding import PartitionSpec as P

MESH = pl.DeviceIdType.MESH
F32 = jnp.float32
BF16 = jnp.bfloat16
NODES = [(0, 0), (1, 0), (0, 1), (1, 1)]
EVEN, ODD = [(0, 0), (1, 0)], [(0, 1), (1, 1)]
PAIRS = [[[(0, 0)], [(1, 0)], [(0, 1)], [(1, 1)]]] * 5
XL, XH, YL, YH = range(4)
SLOTS = [(XL, 0), (XL, 1), (XH, 0), (XH, 1), (YL, None), (YH, None)]
TERMS = 3


def dot(a, b):
    return jnp.dot(a, b, preferred_element_type=F32)


def split(u):
    high = u.astype(BF16)
    return high, (u - high.astype(F32)).astype(BF16)


def dot2(a, u):
    both = dot(a, jnp.concatenate(split(u), axis=1))
    half = u.shape[1]
    return both[:, :half] + both[:, half:]


def shrink_of(square):
    return jnp.where(square > 0.0, jnp.minimum(1.0 / jnp.sqrt(square), 1e12), 1.0)


def extra_of(square):
    return jnp.where(square > 0.0, jnp.minimum(1.0 / jnp.sqrt(square), 1e12), 1e-8)


def fold(a):
    return jnp.sum(a.reshape(-1, 8, a.shape[1]), axis=0)


def over_rows(a):
    return jnp.sum(a, axis=0, keepdims=True)


def kernel(
    ngx, ngy, fast,
    load_ref, blocks_ref, out_ref,
    v, m, t1, t2, reach, lift, up_base, sent, products, halo, first, total, c1, c2, w, scaled_w, scaled_v,
    mine, landed,
    load_sem, halo_send, halo_recv, sum_send, sum_recv, circle,
):
    gx, gy = lax.axis_index("gx"), lax.axis_index("gy")
    up_x, down_x = lax.rem(gx + 1, ngx), lax.rem(gx + ngx - 1, ngx)
    up_y, down_y = lax.rem(gy + 1, ngy), lax.rem(gy + ngy - 1, ngy)
    sides = {XL: (up_x, gy), XH: (down_x, gy), YL: (gx, up_y), YH: (gx, down_y)}
    has_up_x, has_down_x, has_up_y, has_down_y = gx < ngx - 1, gx > 0, gy < ngy - 1, gy > 0
    leaves = {XL: has_up_x, XH: has_down_x, YL: has_up_y, YH: has_down_y}
    arrives = {XL: has_down_x, XH: has_up_x, YL: has_down_y, YH: has_up_y}

    shape = (ngx // fast, fast, ngy // 2, 2)
    z, y, x, core = gx // fast, gx % fast, gy // 2, gy % 2
    chip = x

    def device(offset):
        dz, dy, dx, dc = offset
        return (
            lax.rem(z + dz, shape[0]) * fast + lax.rem(y + dy, shape[1]),
            lax.rem(x + dx, shape[2]) * 2 + lax.rem(core + dc, 2),
        )

    def offsets(*steps):
        wrapped = [tuple(d % n for d, n in zip(step, shape)) for step in steps]
        return [step for step in dict.fromkeys(wrapped) if any(step)]

    ranges = [{8: (5, 4, 3, 2, 1, 6, 7, 0), 4: (1, 2, 3, 0), 2: (1, 0)}.get(n, range(n)) for n in shape]
    groups = [
        [device(step) for step in offsets(*steps)]
        for steps in (
            [(dz, 0, 0, dc) for dz in ranges[0] for dc in ranges[3]],
            [(0, dy, dx, 0) for dy in ranges[1] for dx in ranges[2]],
        )
    ]
    def circle_of(*steps):
        wrapped = [(a % ngx, b % ngy) for a, b in steps]
        return [
            (lax.rem(gx + a, ngx), lax.rem(gy + b, ngy)) for a, b in dict.fromkeys(wrapped) if a or b
        ]

    circles = [
        circle_of((1, 0), (-1, 0), (0, 1), (0, -1)),
        circle_of((2, 0), (-2, 0), (0, 2), (0, -2)),
        circle_of((4, 0), (-4, 0), (0, 4)),
        circle_of((8, 0), (-8, 0)),
        [(gx, chip * 2 + 1 - core)],
    ]

    def tell(number):
        for partner in circles[number]:
            pl.semaphore_signal(circle.at[number], inc=1, device_id=partner, device_id_type=MESH)

    def hear(number):
        if circles[number]:
            pl.semaphore_wait(circle.at[number], len(circles[number]))


    barrier = pltpu.get_barrier_semaphore()
    for partner in sides.values():
        pl.semaphore_signal(barrier, inc=1, device_id=partner, device_id_type=MESH)

    loads = [
        pltpu.make_async_copy(load_ref, v, load_sem.at[0]),
        pltpu.make_async_copy(blocks_ref.at[3], m.at[3], load_sem.at[1]),
        pltpu.make_async_copy(blocks_ref.at[pl.ds(1, 2)], m.at[pl.ds(1, 2)], load_sem.at[2]),
        pltpu.make_async_copy(blocks_ref.at[0], m.at[0], load_sem.at[3]),
    ]
    for copy in loads:
        copy.start()

    arriving = {}

    def send(source, step, side, place=None):
        target = halo.at[side, step] if place is None else halo.at[side, step, place]
        copy = pltpu.make_async_remote_copy(
            src_ref=source,
            dst_ref=target,
            send_sem=halo_send.at[side],
            recv_sem=halo_recv.at[step % 2, SLOTS.index((side, place))],
            device_id=sides[side],
            device_id_type=MESH,
        )
        pl.when(leaves[side])(copy.start)
        arriving[step, side, place] = copy

    def announce(step, i, j):
        if i == 0:
            send(sent.at[step, j, i], step, XH, j)
        if (i, j) == (1, 0):
            send(sent.at[step, j], step, YH)

    def ups(pair):
        return [(0, j, 1, j) for i, j in pair if i == 1] + [(1, i, i, 1) for i, j in pair if j == 1]

    def upward(axis, i, j):
        return t2[i, j] if axis else t1[i, j]

    def pass_up(step, pair, values):
        for (axis, k, i, j), value in zip(ups(pair), values):
            products[step, axis, k] = value.astype(BF16)
        for axis, k, i, j in ups(pair):
            if axis == 0:
                send(products.at[step, 0, k], step, XL, k)
            elif k == 1:
                send(products.at[step, 1], step, YL)

    def reach_of(i, j):
        return [reach[0, j] if i else m[3, i, j], reach[1, i] if j else m[3, i, j]]

    def halos(step, i, j):
        return [halo[XH if i else XL, step, j], halo[YH if j else YL, step, i]]

    def through(matrices, step, i, j):
        across_x, across_y = halos(step, i, j)
        return dot(matrices[0], across_x) + dot(matrices[1], across_y)

    def prepare(field, base):
        for i, j in NODES:
            field[i, j] = base(i, j)
        for axis, k, i, j in ups(NODES):
            up_base[axis, k] = dot(upward(axis, i, j), field[i, j].astype(BF16))

    def exchange(step, field, sign):
        for pair in PAIRS[step]:
            for i, j in pair:
                land(step - 1, i, j)
            for i, j in pair:
                value = field[i, j] + sign * through(reach_of(i, j), step - 1, i, j)
                field[i, j] = value
                sent[step, j, i] = value.astype(BF16)
            values = [
                up_base[axis, k] + sign * through([lift[axis, 0, k], lift[axis, 1, k]], step - 1, i, j)
                for axis, k, i, j in ups(pair)
            ]
            for i, j in pair:
                announce(step, i, j)
            pass_up(step, pair, values)

    def inner(step, field):
        for i, j in NODES:
            value = dot2(m[0, i, j], field[i, j]) if step < 3 else dot(m[0, i, j], sent[step, j, i])
            value += dot(m[1, 0, j], sent[step, j, 1]) if i == 0 else dot(t1[0, j], sent[step, j, 0])
            value += dot(m[2, i, 0], sent[step, 1, i]) if j == 0 else dot(t2[i, 0], sent[step, 0, i])
            total[i, j] = value

    def land(step, i, j):
        keys = [(XH if i else XL, j)]
        if i == 0:
            keys.append((YH if j else YL, None))
        for side, place in keys:
            pl.when(arrives[side])(arriving[step, side, place].wait_recv)

    def outer(step, i, j):
        value = total[i, j]
        value += dot(m[2, i, 1], halo[YH, step, i]) if j else halo[YL, step, i].astype(F32)
        value += dot(m[1, 1, j], halo[XH, step, j]) if i else halo[XL, step, j].astype(F32)
        return value

    def spread(number, phase, rows):
        term = 0
        for row in rows:
            mine[number, phase, pl.ds(term, row.shape[0])] = row
            term += row.shape[0]
        for slot, partner in enumerate(groups[phase]):
            pltpu.make_async_remote_copy(
                src_ref=mine.at[number, phase],
                dst_ref=landed.at[number, phase, slot],
                send_sem=sum_send.at[0],
                recv_sem=sum_recv.at[number, phase],
                device_id=partner,
                device_id_type=MESH,
            ).start()

    def arrive(number, phase):
        pltpu.make_async_remote_copy(
            src_ref=landed.at[number, phase],
            dst_ref=landed.at[number, phase],
            send_sem=sum_send.at[0],
            recv_sem=sum_recv.at[number, phase],
            device_id=groups[phase][0],
            device_id_type=MESH,
        ).wait_recv()
        return [mine[number, phase], *[landed[number, phase, slot] for slot in range(len(groups[phase]))]]

    def joined(parts, to=shrink_of):
        squares, sizes, overlaps = (
            jnp.concatenate([part[term : term + 1] for part in parts], axis=0) for term in range(3)
        )
        square = over_rows(squares)
        ratios = to(square) / shrink_of(squares)
        return [square, over_rows(ratios * ratios * sizes), over_rows(ratios * ratios * overlaps)], ratios, sizes

    def inner_products(*pairs):
        rows = [None] * len(pairs)
        for i, j in NODES:
            for term, (a, b) in enumerate(pairs):
                part = fold(a[i, j] * b[i, j])
                rows[term] = part if rows[term] is None else rows[term] + part
        return [over_rows(row) for row in rows]

    for side in sides:

        @pl.when(jnp.logical_not(arrives[side]))
        def _():
            halo[side] = jnp.zeros(halo.shape[1:], BF16)


    loads[0].wait()
    loads[1].wait()
    for i, j in NODES:
        value = dot2(m[3, i, j], v[i, j])
        first[i, j] = value
        sent[0, j, i] = value.astype(BF16)
    pl.semaphore_wait(barrier, len(sides))
    for i, j in EVEN + ODD:
        announce(0, i, j)
    tell(0)
    loads[2].wait()

    for k in range(2):
        t1[1, k] = m[1, 1, k].T
    for k in range(2):
        t2[k, 1] = m[2, k, 1].T
    pass_up(0, NODES, [dot(upward(axis, i, j), sent[0, j, i]) for axis, k, i, j in ups(NODES)])
    for k in range(2):
        t1[0, k] = m[1, 0, k].T
        t2[k, 0] = m[2, k, 0].T
    loads[3].wait()
    inner(0, first)
    for k in range(2):
        reach[0, k] = dot(m[3, 1, k], m[1, 1, k]).astype(BF16)
        reach[1, k] = dot(m[3, k, 1], m[2, k, 1]).astype(BF16)
    for axis, k, i, j in ups(NODES):
        for side, matrix in enumerate(reach_of(i, j)):
            lift[axis, side, k] = dot(upward(axis, i, j), matrix).astype(BF16)
    prepare(c1, lambda i, j: first[i, j] + dot2(m[3, i, j], v[i, j] - total[i, j]))
    hear(0)
    tell(1)

    exchange(1, c1, -1.0)
    hear(1)
    tell(2)
    inner(1, c1)
    prepare(first, lambda i, j: dot2(m[3, i, j], total[i, j]))
    (square,) = inner_products((v, v))
    shrink = shrink_of(square)
    for i, j in NODES:
        scaled_v[i, j] = v[i, j] * shrink
    hear(2)
    tell(3)

    exchange(2, first, 1.0)
    for i, j in NODES:
        w[i, j] = outer(1, i, j)
    inner(2, first)
    prepare(c2, lambda i, j: first[i, j] + dot2(m[3, i, j], w[i, j] - total[i, j]))
    for i, j in NODES:
        scaled_w[i, j] = w[i, j] * shrink
    sums = [square, *inner_products((scaled_w, scaled_w), (scaled_w, scaled_v))]
    hear(3)
    tell(4)
    hear(4)
    spread(0, 0, sums)

    exchange(3, c2, -1.0)
    inner(3, c2)
    group, _, _ = joined(arrive(0, 0))
    square_of_group, ww, wb = group
    extra = extra_of(ww)
    whole_shrink = shrink_of(square_of_group)
    both = whole_shrink * extra
    ratio = whole_shrink / shrink
    rows = [None] * 3
    for i, j in EVEN + ODD:
        land(3, i, j)
        unit_q = outer(3, i, j) * both
        for term, other in enumerate((scaled_w[i, j], unit_q, scaled_v[i, j])):
            part = fold(other * unit_q)
            rows[term] = part if rows[term] is None else rows[term] + part
    rows = [over_rows(row) for row in rows]
    spread(1, 0, [rows[0] * ratio, rows[1], rows[2] * ratio])
    spread(0, 1, group)
    for side, partner in sides.items():
        all_sent = pltpu.make_async_remote_copy(
            src_ref=halo.at[side],
            dst_ref=halo.at[side],
            send_sem=halo_send.at[side],
            recv_sem=halo_recv.at[0, side],
            device_id=partner,
            device_id_type=MESH,
        )
        pl.when(leaves[side])(all_sent.wait_send)
    spread(1, 1, [functools.reduce(jnp.add, arrive(1, 0))])

    theirs = arrive(0, 1)
    (_, whole_ww, whole_wb), ratios, sizes = joined(theirs, lambda square: 1.0 / jnp.sqrt(square))
    scale = 1.0 / jnp.sqrt(whole_ww)
    extras = scale / extra_of(sizes)
    once = ratios * ratios * extras
    twice = once * extras
    factors = []
    for k in range(len(theirs)):
        row = once[k : k + 1]
        factors.append(jnp.concatenate([row, twice[k : k + 1], row], axis=0))

    last = functools.reduce(jnp.add, [factor * part for factor, part in zip(factors, arrive(1, 1))])
    wq, qq, bq = last[0:1], last[1:2], last[2:3]
    wq = wq * scale
    wb = whole_wb * scale
    second = (bq - wq * wb) / (qq - wq * wq)
    weight_1 = (wb - wq * second) * scale
    weight_2 = second * scale
    for i, j in NODES:
        out_ref[i, j] = weight_1 * c1[i, j] + weight_2 * c2[i, j]
    pltpu.make_async_remote_copy(
        src_ref=landed,
        dst_ref=landed,
        send_sem=sum_send.at[0],
        recv_sem=sum_recv.at[0, 0],
        device_id=groups[0][0],
        device_id_type=MESH,
    ).wait_send()


def solution(mesh):
    ngx, ngy = mesh.shape["gx"], mesh.shape["gy"]
    fast = 4
    others = 2 * (ngx // fast) - 1

    def local(load_vector, blocks):
        cx, cy, size, cases = load_vector.shape
        field = (cx, cy, size, cases)
        matrices = (cx, cy, size, size)
        sem = pltpu.SemaphoreType.DMA
        return pl.pallas_call(
            functools.partial(kernel, ngx, ngy, fast),
            out_shape=jax.ShapeDtypeStruct(field, F32),
            in_specs=[pl.BlockSpec(memory_space=pltpu.HBM)] * 2,
            out_specs=pl.BlockSpec(memory_space=pltpu.VMEM),
            scratch_shapes=[
                pltpu.VMEM(field, F32),
                pltpu.VMEM((4, *matrices), BF16),
                pltpu.VMEM(matrices, BF16),
                pltpu.VMEM(matrices, BF16),
                pltpu.VMEM((2, 2, size, size), BF16),
                pltpu.VMEM((2, 2, 2, size, size), BF16),
                pltpu.VMEM((2, 2, size, cases), F32),
                pltpu.VMEM((4, *field), BF16),
                pltpu.VMEM((4, 2, 2, size, cases), BF16),
                pltpu.VMEM((4, 4, 2, size, cases), BF16),
                pltpu.VMEM(field, F32),
                pltpu.VMEM(field, F32),
                pltpu.VMEM(field, F32),
                pltpu.VMEM(field, F32),
                pltpu.VMEM(field, F32),
                pltpu.VMEM(field, F32),
                pltpu.VMEM(field, F32),
                pltpu.VMEM((2, 2, TERMS, cases), F32),
                pltpu.VMEM((2, 2, others, TERMS, cases), F32),
                sem((4,)),
                sem((4,)),
                sem((2, len(SLOTS))),
                sem((1,)),
                sem((2, 2)),
                pltpu.SemaphoreType.REGULAR((5,)),
            ],
            compiler_params=pltpu.CompilerParams(
                collective_id=0, has_side_effects=True, vmem_limit_bytes=48 * 1024 * 1024
            ),
        )(*[pltpu.with_memory_space_constraint(a, pltpu.HBM) for a in (load_vector, blocks)])

    return jax.shard_map(
        local,
        mesh=mesh,
        in_specs=(P("gx", "gy", None, None), P(None, "gx", "gy", None, None)),
        out_specs=P("gx", "gy", None, None),
        check_vma=False,
    )
```
